128 devices in a mesh: band: 8 (over x_hi, y), tile: 16 (over z, x_lo, core).
Axes of the slice: x: 4 (x_hi: 2, x_lo: 2; x = x_hi * 2 + x_lo), y: 4, z: 4, core: 2. Of those that a mesh axis runs over, the one named last changes fastest.
Arguments:
- regional_state: bfloat16 [128, 512, 512], P('band', 'tile'), may hold values from -60 to 60
- global_state: bfloat16 [128, 256, 1024], P('band', 'tile'), may hold values from -6 to 6
- boundary_cells: int32 [8, 16, 320], P('band', 'tile'), may hold values from -1 to 511, as said below
- source_rows: int32 [8, 16, 16, 64], P('band', 'tile'), may hold values from -1 to 255, as said below
- interp_index: int32 [8, 16, 320, 4], P('band', 'tile'), may hold values from 0 to 1023, as said below
- interp_weights: float32 [8, 16, 320, 4], P('band', 'tile'), may hold values from 0.05 to 0.2
- window_offsets: int32 [2], replicated, may hold values from 1 to 7
- ln_gain: float32 [512], replicated, may hold values from 0.1 to 1.9
- channel_map_weight: bfloat16 [1024, 512], replicated, may hold values from -0.1875 to 0.1875
- qkv_weight: bfloat16 [512, 1536], replicated, may hold values from -0.25 to 0.25
- out_weight: bfloat16 [512, 512], replicated, may hold values from -0.25 to 0.25
- pos_bias: float32 [16, 4096], replicated, may hold values from -6 to 330
- update_cot: bfloat16 [128, 512, 512], P('band', 'tile'), may hold values from -6 to 6
Outputs:
- update: bfloat16 [128, 512, 512], P('band', 'tile')
- regional_grad: bfloat16 [128, 512, 512], P('band', 'tile')
- global_grad: bfloat16 [128, 256, 1024], P('band', 'tile')
The draws below stay inside these ranges and needn't reach their ends.
Inputs may be any that keep to these rules, and one draw needn't show every extreme that they name: `boundary_cells`: for the tile at band b and tile column t: the cells of that tile, numbered y * 32 + x, that lie within 8 cells of the regional domain's edge, each once in no fixed order, then -1 in the remaining slots; the four corner tiles fill all 320 slots. `source_rows`: entry [b, t, o, j] names a global cell of the owner at band b and tile column o, numbered row * 16 + column; live entries of a list are distinct and come first, -1 fills the rest. Only tiles on the regional domain's edge ask; such a tile asks from 4 owners, exactly 64 rows from one of them and 32 to 64 from each other; in the first and the last band every tile asks 64 rows from one owner common to the band. `interp_index`: each entry is o * 64 + j with source_rows[b, t, o, j] live; tiles that ask nothing hold 0.
All inputs are finite; a program needn't handle non-finite values.
Results may differ from the reference program's by a relative error of at most 0.027.
Values may be sent and summed in bfloat16 or wider, within the bound.
A program may use at most 128 MiB of HBM per device.

```python
import jax
import jax.numpy as jnp
from jax import lax

CR = 512
CG = 1024
HEADS = 16
WS = 8
WIN = 64
TY = 16
TX = 32
GL_DEV = 16
GO_DEV = 16
CAP = 64
BW = 8
K = 4
OWN = 4
ZONE = 320
RY = 128
RX = 512
GLAT = 128
GLON = 256
N_BAND = 8
N_TILE = 16


def owner_plan(key):
    plan_key = jax.random.fold_in(key, 7)
    star_key, order_key, count_key = jax.random.split(plan_key, 3)
    band_id = jnp.arange(N_BAND)[:, None]
    tile_id = jnp.arange(N_TILE)[None, :]
    border = (band_id == 0) | (band_id == N_BAND - 1) | (tile_id == 0) | (tile_id == N_TILE - 1)
    common = jax.random.randint(star_key, (N_BAND, 1, 1), 0, N_TILE)
    order_keys = jax.random.split(order_key, N_BAND * N_TILE)
    others = jax.vmap(lambda single: jax.random.permutation(single, N_TILE - 1))(order_keys)
    others = others[:, :OWN - 1].reshape(N_BAND, N_TILE, OWN - 1).astype(jnp.int32)
    others = others + (others >= common).astype(jnp.int32)
    owners = jnp.concatenate([jnp.broadcast_to(common, (N_BAND, N_TILE, 1)).astype(jnp.int32), others], axis=-1)
    extra = jax.random.randint(count_key, (N_BAND, N_TILE, OWN - 1), CAP // 2, CAP + 1)
    counts = jnp.concatenate([jnp.full((N_BAND, N_TILE, 1), CAP, jnp.int32), extra.astype(jnp.int32)], axis=-1)
    counts = counts * border[:, :, None].astype(jnp.int32)
    return (owners, counts)


def draw_source_rows(key, part):
    owners, counts = owner_plan(key)
    key = jax.random.fold_in(key, 1)
    cell_total = GL_DEV * GO_DEV
    per_owner = jnp.sum(counts[..., None] * (owners[..., None] == jnp.arange(N_TILE)).astype(jnp.int32), axis=2)
    row_keys = jax.random.split(key, N_BAND * N_TILE * N_TILE)
    chosen = jax.vmap(lambda single: jax.random.permutation(single, cell_total)[:CAP])(row_keys)
    chosen = chosen.reshape(N_BAND, N_TILE, N_TILE, CAP).astype(jnp.int32)
    first_owner = owners[0, 0, 0]
    listed = chosen[0, 0, first_owner]
    listed = jnp.where(listed == cell_total - 1, listed[0], listed).at[0].set(cell_total - 1)
    chosen = chosen.at[0, 0, first_owner].set(listed)
    return jnp.where(jnp.arange(CAP) < per_owner[..., None], chosen, -1).astype(jnp.int32)


def draw_interp_index(key, part):
    owners, counts = owner_plan(key)
    key = jax.random.fold_in(key, 2)
    pick_key, slot_key = jax.random.split(key)
    shape = (N_BAND, N_TILE, ZONE, K)
    pick = jax.random.randint(pick_key, shape, 0, OWN)
    flat_pick = pick.reshape(N_BAND, N_TILE, -1)
    owner_of = jnp.take_along_axis(owners, flat_pick, axis=-1).reshape(shape)
    count_of = jnp.take_along_axis(counts, flat_pick, axis=-1).reshape(shape)
    slot_of = jax.random.randint(slot_key, shape, 0, jnp.maximum(count_of, 1))
    return jnp.where(count_of > 0, owner_of * CAP + slot_of, 0).astype(jnp.int32)


def draw_boundary_cells(key, part):
    key = jax.random.fold_in(key, 3)
    cell_total = TY * TX
    local = jnp.arange(cell_total)
    band_id = jnp.arange(N_BAND)[:, None, None]
    tile_id = jnp.arange(N_TILE)[None, :, None]
    row_all = band_id * TY + local // TX
    col_all = tile_id * TX + local % TX
    zone = (row_all < BW) | (row_all >= TY * N_BAND - BW) | (col_all < BW) | (col_all >= TX * N_TILE - BW)
    perm_keys = jax.random.split(key, N_BAND * N_TILE)
    shuffled = jax.vmap(lambda single: jax.random.permutation(single, cell_total))(perm_keys)
    shuffled = shuffled.reshape(N_BAND, N_TILE, cell_total).astype(jnp.int32)
    scored = jnp.where(zone, shuffled, cell_total + shuffled)
    ordered = jnp.argsort(scored, axis=-1)[..., :ZONE].astype(jnp.int32)
    in_zone = jnp.arange(ZONE) < jnp.sum(zone.astype(jnp.int32), axis=-1, keepdims=True)
    return jnp.where(in_zone, ordered, -1).astype(jnp.int32)


def draw_regional_state(key, part):
    key = jax.random.fold_in(key, 21)
    base_key = jax.random.fold_in(key, 0)
    values = jax.random.truncated_normal(base_key, -4.5, 4.5, (TY * N_BAND, TX * N_TILE, CR))
    return values.astype(jnp.bfloat16)


def draw_pos_bias(key, part):
    key = jax.random.fold_in(key, 22)
    base_key = jax.random.fold_in(key, 0)
    bias = jax.random.truncated_normal(base_key, -4.0, 4.0, (HEADS, WIN, WIN))
    return bias.reshape(HEADS, WIN * WIN).astype(jnp.float32)


def levels(stream_key, dims, shards, low, top_value):
    factor_of, own = 1.0, jax.random.fold_in(stream_key, 6)
    for dim, shards_of in shards:
        heights = jnp.exp(jax.random.uniform(jax.random.fold_in(own, dim), (shards_of,), jnp.float32, low / len(shards), top_value / len(shards)))
        factor_of = factor_of * jnp.repeat(heights, dims[dim] // shards_of).reshape([-1 if axis == dim else 1 for axis in range(len(dims))])
    return factor_of


def bell_draw(key, shape, spread, reach, cuts=(), held_as=jnp.bfloat16):
    level = levels(key, shape, cuts, -0.22, 0.18) if cuts else 1.0
    drawn = jax.random.normal(key, shape, jnp.float32) * spread * level
    return jnp.minimum(jnp.maximum(drawn, -reach), reach).astype(held_as)


def setup_inputs(seed: int = 0) -> dict:
    key_of = jax.random.split(jax.random.key(seed), 14)
    regional_state = draw_regional_state(jax.random.fold_in(key_of[13], 71), 0)
    global_state = bell_draw(key_of[1], (GLAT, GLON, CG), 1.0, 6.0, ((0, 8), (1, 16)))
    boundary_cells = draw_boundary_cells(jax.random.fold_in(key_of[13], 71), 0)
    source_rows = draw_source_rows(jax.random.fold_in(key_of[13], 71), 0)
    interp_index = draw_interp_index(jax.random.fold_in(key_of[13], 71), 0)
    interp_weights = jnp.clip(0.05 + 0.15 * jax.random.uniform(key_of[5], (N_BAND, N_TILE, ZONE, K), jnp.float32) ** levels(key_of[5], (N_BAND, N_TILE, ZONE, K), ((0, 8), (1, 16)), -0.2, 0.2), 0.05, 0.2)
    window_offsets = jax.random.randint(key_of[6], (2,), 1, WS).astype(jnp.int32)
    ln_gain = jnp.clip(1.0 + 0.18 * jax.random.normal(key_of[7], (CR,), jnp.float32), 0.1, 1.9)
    channel_map_weight = bell_draw(key_of[8], (CG, CR), CG ** -0.5, 0.1875)
    qkv_weight = bell_draw(key_of[9], (CR, 3 * CR), CR ** -0.5, 0.25)
    out_weight = bell_draw(key_of[10], (CR, CR), CR ** -0.5, 0.25)
    pos_bias = draw_pos_bias(jax.random.fold_in(key_of[13], 71), 0)
    update_cot = bell_draw(key_of[12], (RY, RX, CR), 1.0, 6.0, ((0, 8), (1, 16)))
    return dict(regional_state=regional_state, global_state=global_state, boundary_cells=boundary_cells, source_rows=source_rows, interp_index=interp_index, interp_weights=interp_weights, window_offsets=window_offsets, ln_gain=ln_gain, channel_map_weight=channel_map_weight, qkv_weight=qkv_weight, out_weight=out_weight, pos_bias=pos_bias, update_cot=update_cot)


epsilon = 1e-05

def norm_rows(field):
    values = field.astype(jnp.float32)
    middle = lax.optimization_barrier(jnp.mean(values, axis=-1, keepdims=True))
    centred = values - middle
    inverse = lax.rsqrt(lax.optimization_barrier(jnp.mean(centred * centred, axis=-1, keepdims=True)) + epsilon)
    return (centred * inverse, inverse)

def split_windows(field, window, head_count):
    rows_all, cols_all, channels = field.shape
    head_size = channels // head_count
    blocks = field.reshape(rows_all // window, window, cols_all // window, window, head_count, head_size)
    blocks = blocks.transpose(0, 2, 4, 1, 3, 5)
    return blocks.reshape(-1, head_count, window * window, head_size)

def merge_windows(blocks, rows_all, cols_all, window):
    head_count = blocks.shape[1]
    head_size = blocks.shape[3]
    grid = blocks.reshape(rows_all // window, cols_all // window, head_count, window, window, head_size)
    return grid.transpose(0, 3, 1, 4, 2, 5).reshape(rows_all, cols_all, head_count * head_size)

def local_window_attend(field, cotangent, inside, ln_gain, qkv_weight, out_weight, pos_bias, window):
    rows_all, cols_all, channels = field.shape
    head_count = pos_bias.shape[0]
    head_size = channels // head_count
    size_w = window * window
    normal, unused = norm_rows(field)
    normed = (normal * ln_gain).astype(jnp.bfloat16)
    qkv = jnp.dot(normed.reshape(-1, channels), qkv_weight, preferred_element_type=jnp.float32)
    qkv = qkv.astype(jnp.bfloat16).reshape(rows_all, cols_all, 3 * channels)
    queries = split_windows(qkv[..., :channels], window, head_count).astype(jnp.float32)
    keys_win = split_windows(qkv[..., channels:2 * channels], window, head_count).astype(jnp.float32)
    values_win = split_windows(qkv[..., 2 * channels:], window, head_count).astype(jnp.float32)
    key_mask = split_windows(inside[:, :, None], window, 1)[:, :, None, :, 0]
    bias = pos_bias.reshape(head_count, size_w, size_w)
    scale_factor = head_size ** (-0.5)
    scores = jnp.einsum('whid,whjd->whij', queries, keys_win) * scale_factor + bias
    scores = jnp.where(key_mask, scores, -1e+30)
    peak = lax.optimization_barrier(jnp.max(scores, axis=-1, keepdims=True))
    raised = jnp.exp(scores - peak)
    chances = raised / lax.optimization_barrier(jnp.sum(raised, axis=-1, keepdims=True))
    reduced_probability = chances.astype(jnp.bfloat16)
    context = jnp.einsum('whij,whjd->whid', reduced_probability.astype(jnp.float32), values_win).astype(jnp.bfloat16)
    context_grid = merge_windows(context, rows_all, cols_all, window).reshape(-1, channels)
    update = jnp.dot(context_grid, out_weight, preferred_element_type=jnp.float32).astype(jnp.bfloat16)
    update = update.reshape(rows_all, cols_all, channels)
    grad_context = jnp.dot(cotangent.reshape(-1, channels), out_weight.T, preferred_element_type=jnp.float32)
    grad_context = grad_context.astype(jnp.bfloat16).reshape(rows_all, cols_all, channels)
    grad_win = split_windows(grad_context, window, head_count).astype(jnp.float32)
    grad_chances = jnp.einsum('whid,whjd->whij', grad_win, values_win)
    grad_scores = chances * (grad_chances - lax.optimization_barrier(jnp.sum(chances * grad_chances, axis=-1, keepdims=True)))
    grad_low = (grad_scores * scale_factor).astype(jnp.bfloat16).astype(jnp.float32)
    query_gradient = jnp.einsum('whij,whjd->whid', grad_low, keys_win).astype(jnp.bfloat16)
    grad_key = jnp.einsum('whij,whid->whjd', grad_low, queries).astype(jnp.bfloat16)
    grad_value = jnp.einsum('whij,whid->whjd', reduced_probability.astype(jnp.float32), grad_win).astype(jnp.bfloat16)
    grad_qkv = jnp.concatenate([merge_windows(query_gradient, rows_all, cols_all, window), merge_windows(grad_key, rows_all, cols_all, window), merge_windows(grad_value, rows_all, cols_all, window)], axis=-1)
    return (update, grad_qkv)

def ln_backward(field, grad_qkv, ln_gain, qkv_weight):
    channels = field.shape[-1]
    normal, inverse = norm_rows(field.reshape(-1, channels))
    grad_normed = jnp.dot(grad_qkv.reshape(-1, 3 * channels), qkv_weight.T, preferred_element_type=jnp.float32)
    scaled = grad_normed * ln_gain
    return inverse * (scaled - lax.optimization_barrier(jnp.mean(scaled, axis=-1, keepdims=True)) - normal * lax.optimization_barrier(jnp.mean(scaled * normal, axis=-1, keepdims=True)))

def reference(regional_state, global_state, boundary_cells, source_rows, interp_index, interp_weights, window_offsets, ln_gain, channel_map_weight, qkv_weight, out_weight, pos_bias, update_cot):
    channels = regional_state.shape[-1]
    global_width = global_state.shape[-1]
    rows_all = TY * N_BAND
    cols_all = TX * N_TILE
    global_cols = GO_DEV * N_TILE
    band_id = jnp.arange(N_BAND, dtype=jnp.int32)
    tile_id = jnp.arange(N_TILE, dtype=jnp.int32)
    in_use = source_rows >= 0
    local_row = jnp.maximum(source_rows, 0)
    global_cell = (band_id[:, None, None, None] * GL_DEV + local_row // GO_DEV) * global_cols + tile_id[None, None, :, None] * GO_DEV + local_row % GO_DEV
    global_flat = global_state.reshape(-1, global_width)
    projected = jnp.dot(global_flat, channel_map_weight, preferred_element_type=jnp.float32).astype(jnp.bfloat16)
    fetched = jnp.where(in_use[..., None], projected[global_cell], jnp.zeros((), jnp.bfloat16))
    fetched = fetched.reshape(-1, channels)
    device_base = ((band_id[:, None] * N_TILE + tile_id[None, :]) * (N_TILE * CAP))[:, :, None, None]
    fetch_index = device_base + interp_index
    gathered = fetched[fetch_index].astype(jnp.float32)
    interpolated = jnp.einsum('btzk,btzkc->btzc', interp_weights, gathered)
    relax = lax.optimization_barrier(jnp.sum(interp_weights, axis=-1))
    zone_live = boundary_cells >= 0
    zone_local = jnp.maximum(boundary_cells, 0)
    zone_global = (band_id[:, None, None] * TY + zone_local // TX) * cols_all + tile_id[None, :, None] * TX + zone_local % TX
    state_flat = regional_state.reshape(-1, channels)
    current = state_flat[zone_global].astype(jnp.float32)
    blended = ((1.0 - relax)[..., None] * current + interpolated).astype(jnp.bfloat16)
    zone_target = jnp.where(zone_live, zone_global, rows_all * cols_all).reshape(-1)
    filled = state_flat.at[zone_target].set(blended.reshape(-1, channels), mode='drop')
    filled = filled.reshape(rows_all, cols_all, channels)
    offset_y = window_offsets[0]
    offset_x = window_offsets[1]
    zero_index = jnp.zeros((), jnp.int32)
    margin = ((WS, WS), (WS, WS), (0, 0))
    extent = (rows_all + WS, cols_all + WS, channels)
    field = lax.dynamic_slice(jnp.pad(filled, margin), (offset_y, offset_x, zero_index), extent)
    cotangent = lax.dynamic_slice(jnp.pad(update_cot, margin), (offset_y, offset_x, zero_index), extent)
    row_coord = offset_y - WS + jnp.arange(rows_all + WS, dtype=jnp.int32)
    col_coord = offset_x - WS + jnp.arange(cols_all + WS, dtype=jnp.int32)
    inside = ((row_coord >= 0) & (row_coord < rows_all))[:, None] & ((col_coord >= 0) & (col_coord < cols_all))[None, :]
    strips = rows_all // WS + 1

    def single_latitude_slice(pieces):
        return local_window_attend(pieces[0], pieces[1], pieces[2], ln_gain, qkv_weight, out_weight, pos_bias, WS)
    update_ext, grad_ext = lax.map(single_latitude_slice, (field.reshape(strips, WS, cols_all + WS, channels), cotangent.reshape(strips, WS, cols_all + WS, channels), inside.reshape(strips, WS, cols_all + WS)))
    update_ext = update_ext.reshape(rows_all + WS, cols_all + WS, channels)
    grad_ext = grad_ext.reshape(rows_all + WS, cols_all + WS, 3 * channels)
    start = (WS - offset_y, WS - offset_x, zero_index)
    update = lax.dynamic_slice(update_ext, start, (rows_all, cols_all, channels))
    grad_qkv = lax.dynamic_slice(grad_ext, start, (rows_all, cols_all, 3 * channels))
    grad_filled = ln_backward(filled, grad_qkv, ln_gain, qkv_weight)
    grad_zone = jnp.where(zone_live[..., None], grad_filled[zone_global], 0.0)
    regional_grad = grad_filled.at[zone_target].set(((1.0 - relax)[..., None] * grad_zone).reshape(-1, channels), mode='drop')
    regional_grad = regional_grad.astype(jnp.bfloat16).reshape(rows_all, cols_all, channels)
    grad_fetched = jnp.zeros((N_BAND * N_TILE * N_TILE * CAP, channels), jnp.float32)
    for column in range(K):
        grad_fetched = grad_fetched.at[fetch_index[..., column].reshape(-1)].add((interp_weights[..., column, None] * grad_zone).reshape(-1, channels))
    grad_fetched = grad_fetched.astype(jnp.bfloat16)
    global_cells = global_flat.shape[0]
    owner_target = jnp.where(in_use, global_cell, global_cells).reshape(-1)
    gathered_grad = jnp.zeros((global_cells, channels), jnp.float32).at[owner_target].add(grad_fetched.astype(jnp.float32), mode='drop')
    global_grad = jnp.dot(gathered_grad, channel_map_weight.astype(jnp.float32).T, precision=lax.Precision.HIGHEST)
    global_grad = global_grad.astype(jnp.bfloat16).reshape(global_state.shape)
    return (update, regional_grad, global_grad)
```

```python
import functools

import jax
import jax.numpy as jnp
from jax import lax
from jax.experimental import pallas as pl
from jax.experimental.pallas import tpu as pltpu
from jax.sharding import PartitionSpec as P

WS = 8
C = 512
HEADS = 16
GROUPS = 4
WY = 3
WX = 5
STRIP = WX * 64
EPS = 1e-05
BF = jnp.bfloat16
F32 = jnp.float32


def dot(a, b, dims=((1,), (0,))):
    return lax.dot_general(a, b, (dims, ((), ())), preferred_element_type=F32)


def norm_rows(x):
    centred = x - jnp.mean(x, axis=-1, keepdims=True)
    inverse = lax.rsqrt(jnp.mean(centred * centred, axis=-1, keepdims=True) + EPS)
    return centred * inverse, inverse


def block_diagonal(x):
    lane = lax.broadcasted_iota(jnp.int32, x.shape, 1) // 32
    return jnp.concatenate([jnp.where(lane == h, x, jnp.zeros_like(x)) for h in range(4)], axis=0)


def diagonal_blocks(x):
    lane = lax.broadcasted_iota(jnp.int32, (64, 128), 1) // 32
    out = x[192:256]
    for h in (2, 1, 0):
        out = jnp.where(lane == h, x[64 * h : 64 * h + 64], out)
    return out


def middle_kernel(
    off_ref, filled_ref, frow_ref, fside_ref, fcorner_ref, pside_ref, prow_ref, cot_ref, crow_ref, cside_ref, ccorner_ref,
    gain_ref, wqkv_ref, wout_ref, bias_ref, at_ref, keep_ref,
    update_ref, rgrad_ref, gfetch_ref,
    fext, cext, normed, cotw, qkv, gctx, ctx, gqkv, upd, gx, gfb,
):
    band, tile = lax.axis_index("band"), lax.axis_index("tile")
    oy, ox = off_ref[0], off_ref[1]
    has = (band > 0, band < 7, tile > 0, tile < 15)

    def clean(x, ok):
        return jnp.where(ok, x.astype(F32), 0.0)

    def build(ext, own, row, side, corner):
        @pl.loop(0, 16)
        def _(y):
            ext[8 + y, 0:32] = own[y].astype(F32)

        @pl.loop(0, 8)
        def _(y):
            ext[y, 0:32] = clean(row[0, y], has[0])
            ext[24 + y, 0:32] = clean(row[1, y], has[1])
            for s in range(2):
                both = clean(side[s, y], has[2 + s])
                place = slice(40, 48) if s == 0 else slice(32, 40)
                ext[8 + y, place] = both[0:8]
                ext[16 + y, place] = both[8:16]

        @pl.loop(0, 4)
        def _(y):
            for v in range(2):
                for s in range(2):
                    both = clean(corner[2 * v + s, y], has[v] & has[2 + s])
                    place = slice(40, 48) if s == 0 else slice(32, 40)
                    ext[24 * v + y, place] = both[0:8]
                    ext[24 * v + 4 + y, place] = both[8:16]

    build(fext, filled_ref, frow_ref, fside_ref, fcorner_ref)
    build(cext, cot_ref, crow_ref, cside_ref, ccorner_ref)

    for s in range(2):
        place = slice(40, 48) if s == 0 else slice(32, 40)
        for here, top in ((band == 0, 0), (band == 7, 8)):
            @pl.when(here)
            def _(s=s, place=place, top=top):
                for y in range(4):
                    both = clean(pside_ref[s, y], has[2 + s])
                    fext[8 + top + y, place] = both[0:8]
                    fext[12 + top + y, place] = both[8:16]
        for here, left in ((tile == 0, 0), (tile == 15, 24)):
            @pl.when(here)
            def _(s=s, left=left):
                for y in range(4):
                    both = clean(prow_ref[s, y], has[s])
                    fext[24 * s + y, left : left + 8] = both[0:8]
                    fext[24 * s + 4 + y, left : left + 8] = both[8:16]

    gain = gain_ref[...]

    def strip(wy, carry):
        def pair(p, carry):
            base = pl.multiple_of(wy * STRIP + p * 16, 16)
            r = oy + wy * 8 + p * 2
            for src, dst, norm in ((fext, normed, True), (cext, cotw, False)):
                rows = []
                for q in range(2):
                    x = pltpu.roll(src[r + q], 8 - ox, 0)[0:40]
                    if norm:
                        x = norm_rows(x)[0] * gain
                    rows.append(x)
                for wx in range(WX):
                    piece = jnp.concatenate([rows[0][8 * wx : 8 * wx + 8], rows[1][8 * wx : 8 * wx + 8]], axis=0)
                    dst[pl.ds(pl.multiple_of(base + wx * 64, 16), 16), :] = piece.astype(BF)
            return carry

        lax.fori_loop(0, 4, pair, 0)
        cells = pl.ds(pl.multiple_of(wy * STRIP, 16), STRIP)
        x = normed[cells, :]
        for n in range(6):
            qkv[cells, 256 * n : 256 * n + 256] = dot(x, wqkv_ref[:, 256 * n : 256 * n + 256]).astype(BF)
        x = cotw[cells, :]
        for n in range(2):
            gctx[cells, 256 * n : 256 * n + 256] = dot(x, wout_ref[256 * n : 256 * n + 256, :], ((1,), (1,))).astype(BF)
        return carry

    lax.fori_loop(0, WY, strip, 0)

    scale = 32 ** (-0.5)

    def window(w, carry):
        wy, wx = w // WX, w % WX
        cells = pl.ds(pl.multiple_of(w * 64, 64), 64)
        j = lax.broadcasted_iota(jnp.int32, (64, 1), 0)
        ry = band * 16 + oy - 8 + wy * 8 + j // 8
        rx = tile * 32 + ox - 8 + wx * 8 + j % 8
        inside = (ry >= 0) & (ry < 128) & (rx >= 0) & (rx < 512)
        shut = jnp.where(inside, 0.0, -1e30)
        for g in range(GROUPS):
            lo = 128 * g
            q = qkv[cells, lo : lo + 128]
            k = qkv[cells, 512 + lo : 512 + lo + 128]
            v = qkv[cells, 1024 + lo : 1024 + lo + 128]
            go = gctx[cells, lo : lo + 128]
            qb, gb = block_diagonal(q), block_diagonal(go)
            s = dot(k, qb, ((1,), (1,))) * scale + (bias_ref[g] + shut)
            e = jnp.exp(s - jnp.max(s, axis=0, keepdims=True))
            p = e / jnp.sum(e, axis=0, keepdims=True)
            pb = p.astype(BF)
            gp = dot(v, gb, ((1,), (1,)))
            gs = p * (gp - jnp.sum(p * gp, axis=0, keepdims=True))
            gl = (gs * scale).astype(BF)
            ctx[cells, lo : lo + 128] = diagonal_blocks(dot(pb, v, ((0,), (0,)))).astype(BF)
            gqkv[cells, lo : lo + 128] = diagonal_blocks(dot(gl, k, ((0,), (0,)))).astype(BF)
            gqkv[cells, 512 + lo : 512 + lo + 128] = dot(gl, qb).astype(BF)
            gqkv[cells, 1024 + lo : 1024 + lo + 128] = dot(pb, gb).astype(BF)
        return carry

    lax.fori_loop(0, WY * WX, window, 0)

    def back(wy, carry):
        cells = pl.ds(pl.multiple_of(wy * STRIP, 16), STRIP)
        for n in range(2):
            cols = slice(256 * n, 256 * n + 256)
            u = dot(ctx[cells, :], wout_ref[:, cols])
            g = dot(gqkv[cells, :], wqkv_ref[cols, :], ((1,), (1,)))
            for wx in range(WX):
                for iy in range(8):
                    at = 64 * wx + 8 * iy
                    upd[8 * wy + iy, 8 * wx : 8 * wx + 8, cols] = u[at : at + 8]
                    gx[8 * wy + iy, 8 * wx : 8 * wx + 8, cols] = g[at : at + 8]
        return carry

    lax.fori_loop(0, WY, back, 0)

    def tail(y, carry):
        r = y + 8 - oy
        update_ref[y] = pltpu.roll(upd[r], 32 + ox, 0)[0:32].astype(BF)
        p = pltpu.roll(gx[r], 32 + ox, 0)[0:32] * gain
        normal, inverse = norm_rows(filled_ref[y].astype(F32))
        g = inverse * (
            p - jnp.mean(p, axis=-1, keepdims=True) - normal * jnp.mean(p * normal, axis=-1, keepdims=True)
        )
        at = pl.ds(pl.multiple_of(y * 32, 32), 32)
        rgrad_ref[y] = (g * keep_ref[at, 0:1]).astype(BF)
        gfb[at, :] = g.astype(BF)
        return carry

    lax.fori_loop(0, 16, tail, 0)
    for n in range(2):
        cols = slice(256 * n, 256 * n + 256)
        g = gfb[:, cols]
        for m in range(4):
            gfetch_ref[256 * m : 256 * m + 256, cols] = dot(at_ref[256 * m : 256 * m + 256, :], g).astype(BF)


def middle(off, filled, frow, fside, fcorner, pside, prow, cot, crow, cside, ccorner, gain, wqkv, wout, bias, at, keep):
    vm = pl.BlockSpec(memory_space=pltpu.VMEM)
    return pl.pallas_call(
        middle_kernel,
        out_shape=(
            jax.ShapeDtypeStruct((16, 32, C), BF),
            jax.ShapeDtypeStruct((16, 32, C), BF),
            jax.ShapeDtypeStruct((1024, C), BF),
        ),
        in_specs=[pl.BlockSpec(memory_space=pltpu.SMEM)] + [vm] * 16,
        out_specs=(vm, vm, vm),
        scratch_shapes=[
            pltpu.VMEM((32, 48, C), F32),
            pltpu.VMEM((32, 48, C), F32),
            pltpu.VMEM((960, C), BF),
            pltpu.VMEM((960, C), BF),
            pltpu.VMEM((960, 3 * C), BF),
            pltpu.VMEM((960, C), BF),
            pltpu.VMEM((960, C), BF),
            pltpu.VMEM((960, 3 * C), BF),
            pltpu.VMEM((24, 40, C), F32),
            pltpu.VMEM((24, 40, C), F32),
            pltpu.VMEM((512, C), BF),
        ],
        compiler_params=pltpu.CompilerParams(vmem_limit_bytes=56 * 2**20),
        cost_estimate=pl.CostEstimate(flops=6 * 10**9, bytes_accessed=8 * 10**6, transcendentals=10**6),
    )(off, filled, frow, fside, fcorner, pside, prow, cot, crow, cside, ccorner, gain, wqkv, wout, bias, at, keep)


MESH = pl.DeviceIdType.MESH
PEERS = 15
HALO = tuple((dv, ds) for dv in (-1, 0, 1) for ds in (-1, 0, 1) if (dv, ds) != (0, 0))


def one_hot_rows(row):
    cell = lax.broadcasted_iota(jnp.int32, (256, 64), 0)
    return (cell == row).astype(F32).astype(BF)


def front_kernel(
    global_ref, cmap_ref, src_ref, bc_ref, idx_ref, w_ref, state_ref, cot_ref,
    filled_ref, frow, fside, fcorner, crow, cside, ccorner, pside, prow, at_ref, keep_ref, asked,
    fetched, outbox, proj, bt, amat, sidebox, cornerbox, patchbox,
    req_send, req_recv, row_send, row_recv, halo_send, halo_recv, patch_send, patch_recv,
):
    band, me = lax.axis_index("band"), lax.axis_index("tile")

    def place(dv, ds):
        return (lax.rem(band + 8 + dv, 8), lax.rem(me + 16 + ds, 16))

    barrier = pltpu.get_barrier_semaphore()
    for d in range(1, PEERS + 1):
        pl.semaphore_signal(barrier, inc=1, device_id=(band, me ^ d), device_id_type=MESH)
    for dv, ds in HALO:
        if dv:
            pl.semaphore_signal(barrier, inc=1, device_id=place(dv, ds), device_id_type=MESH)
    pl.semaphore_wait(barrier, PEERS + 6)

    def request(d):
        return pltpu.make_async_remote_copy(
            src_ref=src_ref.at[me ^ d], dst_ref=asked.at[me], send_sem=req_send.at[d], recv_sem=req_recv.at[d],
            device_id=(band, me ^ d), device_id_type=MESH,
        )

    for d in range(1, PEERS + 1):
        request(d).start()
    asked[me] = src_ref[me]

    def halo(which, h, dv, ds):
        own = state_ref if which == 0 else cot_ref
        rows, sides, corners = ((frow, fside, fcorner), (crow, cside, ccorner))[which]
        v, s = (0 if dv == 1 else 1), (0 if ds == 1 else 1)
        if ds == 0:
            src, dst = own.at[0:8] if dv == -1 else own.at[8:16], rows.at[v]
        elif dv == 0:
            src, dst = sidebox.at[2 * which + s], sides.at[s]
        else:
            src, dst = cornerbox.at[4 * which + 2 * v + s], corners.at[2 * v + s]
        return pltpu.make_async_remote_copy(
            src_ref=src, dst_ref=dst, send_sem=halo_send.at[8 * which + h], recv_sem=halo_recv.at[8 * which + h],
            device_id=place(dv, ds), device_id_type=MESH,
        )

    def two(a, b):
        return jnp.concatenate([a.astype(F32), b.astype(F32)], axis=0).astype(BF)

    for which, own in ((1, cot_ref), (0, state_ref)):
        for s in range(2):
            cols = slice(24, 32) if s == 0 else slice(0, 8)
            for y in range(8):
                sidebox[2 * which + s, y] = two(own[y][cols], own[y + 8][cols])
            for v in range(2):
                top = 8 if v == 0 else 0
                for y in range(4):
                    cornerbox[4 * which + 2 * v + s, y] = two(own[top + y][cols], own[top + y + 4][cols])
        for h, (dv, ds) in enumerate(HALO):
            halo(which, h, dv, ds).start()

    for n in range(2):
        cols = slice(256 * n, 256 * n + 256)
        proj[:, cols] = dot(global_ref[...], cmap_ref[:, cols]).astype(BF)

    def send_row(d):
        return pltpu.make_async_remote_copy(
            src_ref=outbox.at[me ^ d], dst_ref=fetched.at[me], send_sem=row_send.at[d], recv_sem=row_recv.at[d],
            device_id=(band, me ^ d), device_id_type=MESH,
        )

    def serve(d, carry):
        request(d).wait_recv()
        hot = one_hot_rows(asked[me ^ d])
        outbox[me ^ d] = dot(hot, proj[...], ((0,), (0,))).astype(BF)
        send_row(d).start()
        return carry

    lax.fori_loop(1, PEERS + 1, serve, 0)
    fetched[me] = dot(one_hot_rows(asked[me]), proj[...], ((0,), (0,))).astype(BF)

    cell = lax.broadcasted_iota(jnp.int32, (512, 320), 0)
    hit = cell == bc_ref[...]
    weights = w_ref[...]
    relax = jnp.sum(weights, axis=0, keepdims=True)
    spread = jnp.sum(jnp.where(hit, relax, 0.0), axis=1, keepdims=True)
    keep_ref[...] = jnp.broadcast_to(1.0 - spread, (512, 128))
    hit = hit.astype(F32).astype(BF)

    def taps(m, carry):
        at = pl.ds(pl.multiple_of(m * 128, 128), 128)
        f = lax.broadcasted_iota(jnp.int32, (128, 320), 0) + m * 128
        total = jnp.zeros((128, 320), F32)
        for k in range(4):
            total = total + jnp.where(idx_ref[k : k + 1, :] == f, w_ref[k : k + 1, :], 0.0)
        bt[at, :] = total.astype(BF)
        at_ref[at, :] = dot(total.astype(BF), hit, ((1,), (1,))).astype(BF)
        return carry

    lax.fori_loop(0, 8, taps, 0)
    for m in range(4):
        at = slice(256 * m, 256 * m + 256)
        amat[:, at] = dot(hit, bt[at, :], ((1,), (1,))).astype(BF)

    def arrive(d, carry):
        send_row(d).wait_recv()
        return carry

    lax.fori_loop(1, PEERS + 1, arrive, 0)

    for n in range(2):
        cols = slice(256 * n, 256 * n + 256)
        rows = jnp.concatenate([fetched[o, :, cols] for o in range(16)], axis=0)
        for y in range(4):
            at = slice(128 * y, 128 * y + 128)
            own = state_ref[4 * y : 4 * y + 4, :, cols].reshape(128, 256).astype(F32)
            x = own * keep_ref[at, 0:1] + dot(amat[at, :], rows)
            filled_ref[4 * y : 4 * y + 4, :, cols] = x.astype(BF).reshape(4, 32, 256)

    def patch(n):
        s = n % 2
        if n < 2:
            dst, to = pside.at[s], place(0, 1 if s == 0 else -1)
        else:
            dst, to = prow.at[s], place(1 if s == 0 else -1, 0)
        return pltpu.make_async_remote_copy(
            src_ref=patchbox.at[n], dst_ref=dst, send_sem=patch_send.at[n], recv_sem=patch_recv.at[n],
            device_id=to, device_id_type=MESH,
        )

    def patches(top, left, first):
        for s in range(2):
            if first == 0:
                y0, x0 = top, (24 if s == 0 else 0)
            else:
                y0, x0 = (8 if s == 0 else 0), left
            for y in range(4):
                patchbox[first + s, y] = two(
                    filled_ref[y0 + y][x0 : x0 + 8], filled_ref[y0 + y + 4][x0 : x0 + 8]
                )
            patch(first + s).start()

    for here, top in ((band == 0, 0), (band == 7, 8)):
        @pl.when(here)
        def _(top=top):
            patches(top, 0, 0)

    for here, left in ((me == 0, 0), (me == 15, 24)):
        @pl.when(here)
        def _(left=left):
            patches(0, left, 2)

    for which in (1, 0):
        for h, (dv, ds) in enumerate(HALO):
            halo(which, h, dv, ds).wait()
    for d in range(1, PEERS + 1):
        request(d).wait_send()
        send_row(d).wait_send()

    for here, first in (((band == 0) | (band == 7), 0), ((me == 0) | (me == 15), 2)):
        @pl.when(here)
        def _(first=first):
            patch(first).wait()
            patch(first + 1).wait()


def front(state, global_state, bc, src, idx, w, cmap, cot):
    vm = pl.BlockSpec(memory_space=pltpu.VMEM)
    hbm = pl.BlockSpec(memory_space=pl.ANY)
    return pl.pallas_call(
        front_kernel,
        out_shape=(
            jax.ShapeDtypeStruct((16, 32, C), BF),
            jax.ShapeDtypeStruct((2, 8, 32, C), BF),
            jax.ShapeDtypeStruct((2, 8, 16, C), BF),
            jax.ShapeDtypeStruct((4, 4, 16, C), BF),
            jax.ShapeDtypeStruct((2, 8, 32, C), BF),
            jax.ShapeDtypeStruct((2, 8, 16, C), BF),
            jax.ShapeDtypeStruct((4, 4, 16, C), BF),
            jax.ShapeDtypeStruct((2, 4, 16, C), BF),
            jax.ShapeDtypeStruct((2, 4, 16, C), BF),
            jax.ShapeDtypeStruct((1024, C), BF),
            jax.ShapeDtypeStruct((512, 128), F32),
            jax.ShapeDtypeStruct((16, 1, 64), jnp.int32),
        ),
        in_specs=[vm] * 8,
        out_specs=(vm,) + (hbm,) * 8 + (vm, vm, vm),
        scratch_shapes=[
            pltpu.VMEM((16, 64, C), BF),
            pltpu.VMEM((16, 64, C), BF),
            pltpu.VMEM((256, C), BF),
            pltpu.VMEM((1024, 320), BF),
            pltpu.VMEM((512, 1024), BF),
            pltpu.VMEM((4, 8, 16, C), BF),
            pltpu.VMEM((8, 4, 16, C), BF),
            pltpu.VMEM((4, 4, 16, C), BF),
            pltpu.SemaphoreType.DMA((16,)),
            pltpu.SemaphoreType.DMA((16,)),
            pltpu.SemaphoreType.DMA((16,)),
            pltpu.SemaphoreType.DMA((16,)),
            pltpu.SemaphoreType.DMA((16,)),
            pltpu.SemaphoreType.DMA((16,)),
            pltpu.SemaphoreType.DMA((4,)),
            pltpu.SemaphoreType.DMA((4,)),
        ],
        compiler_params=pltpu.CompilerParams(
            collective_id=0, has_side_effects=True, vmem_limit_bytes=48 * 2**20
        ),
    )(global_state, cmap, src, bc, idx, w, state, cot)


def back_kernel(gfetch_ref, asked_ref, cmap_ref, out_ref, landed, send, recv):
    band, me = lax.axis_index("band"), lax.axis_index("tile")
    barrier = pltpu.get_barrier_semaphore()
    for d in range(1, PEERS + 1):
        pl.semaphore_signal(barrier, inc=1, device_id=(band, me ^ d), device_id_type=MESH)
    pl.semaphore_wait(barrier, PEERS)

    def send_row(d):
        return pltpu.make_async_remote_copy(
            src_ref=gfetch_ref.at[me ^ d], dst_ref=landed.at[me], send_sem=send.at[d], recv_sem=recv.at[d],
            device_id=(band, me ^ d), device_id_type=MESH,
        )

    for d in range(1, PEERS + 1):
        send_row(d).start()
    landed[me] = gfetch_ref[me]

    def take(d, total):
        send_row(d).wait_recv()
        return total + dot(one_hot_rows(asked_ref[me ^ d]), landed[me ^ d])

    total = dot(one_hot_rows(asked_ref[me]), landed[me])
    total = lax.fori_loop(1, PEERS + 1, take, total)
    high = total.astype(BF)
    low = (total - high.astype(F32)).astype(BF)
    for n in range(4):
        at = slice(256 * n, 256 * n + 256)
        m = cmap_ref[at, :]
        out_ref[:, at] = (dot(high, m, ((1,), (1,))) + dot(low, m, ((1,), (1,)))).astype(BF)
    for d in range(1, PEERS + 1):
        send_row(d).wait_send()


def back(gfetch, asked, cmap):
    vm = pl.BlockSpec(memory_space=pltpu.VMEM)
    return pl.pallas_call(
        back_kernel,
        out_shape=jax.ShapeDtypeStruct((256, 1024), BF),
        in_specs=[vm] * 3,
        out_specs=vm,
        scratch_shapes=[
            pltpu.VMEM((16, 64, C), BF),
            pltpu.SemaphoreType.DMA((16,)),
            pltpu.SemaphoreType.DMA((16,)),
        ],
        compiler_params=pltpu.CompilerParams(
            collective_id=1, has_side_effects=True, vmem_limit_bytes=32 * 2**20
        ),
    )(gfetch, asked, cmap)


def shards(
    regional_state, global_state, boundary_cells, source_rows, interp_index, interp_weights, window_offsets,
    ln_gain, channel_map_weight, qkv_weight, out_weight, pos_bias, update_cot,
):
    idx = interp_index.reshape(320, 4).T
    w = interp_weights.reshape(320, 4).T
    bias = pos_bias.reshape(4, 4, 64, 64).transpose(0, 3, 1, 2).reshape(4, 64, 256)
    filled, frow, fside, fcorner, crow, cside, ccorner, pside, prow, at, keep, asked = front(
        regional_state, global_state.reshape(256, 1024), boundary_cells.reshape(1, 320),
        source_rows.reshape(16, 1, 64), idx, w, channel_map_weight, update_cot,
    )
    update, rgrad, gfetch = middle(
        window_offsets, filled, frow, fside, fcorner, pside, prow, update_cot, crow, cside, ccorner,
        ln_gain.reshape(1, C), qkv_weight, out_weight, bias, at, keep,
    )
    ggrad = back(gfetch.reshape(16, 64, C), asked, channel_map_weight)
    return update, rgrad, ggrad.reshape(16, 16, 1024)


def solution(mesh):
    tiled = P("band", "tile", None)
    deep = P("band", "tile", None, None)
    return jax.shard_map(
        shards,
        mesh=mesh,
        in_specs=(tiled, tiled, tiled, deep, deep, deep, P(), P(), P(), P(), P(), P(), tiled),
        out_specs=(tiled, tiled, tiled),
        check_vma=False,
    )
```

```python
import functools

import jax
import jax.numpy as jnp
from jax import lax
from jax.experimental import pallas as pl
from jax.experimental.pallas import tpu as pltpu
from jax.sharding import PartitionSpec as P

WS = 8
C = 512
HEADS = 16
GROUPS = 4
WY = 3
WX = 5
STRIP = WX * 64
EPS = 1e-05
BF = jnp.bfloat16
F32 = jnp.float32


def dot(a, b, dims=((1,), (0,))):
    return lax.dot_general(a, b, (dims, ((), ())), preferred_element_type=F32)


def norm_rows(x):
    centred = x - jnp.mean(x, axis=-1, keepdims=True)
    inverse = lax.rsqrt(jnp.mean(centred * centred, axis=-1, keepdims=True) + EPS)
    return centred * inverse, inverse


def block_diagonal(x):
    lane = lax.broadcasted_iota(jnp.int32, x.shape, 1) // 32
    return jnp.concatenate([jnp.where(lane == h, x, jnp.zeros_like(x)) for h in range(4)], axis=0)


def diagonal_blocks(x):
    lane = lax.broadcasted_iota(jnp.int32, (64, 128), 1) // 32
    out = x[192:256]
    for h in (2, 1, 0):
        out = jnp.where(lane == h, x[64 * h : 64 * h + 64], out)
    return out


MESH = pl.DeviceIdType.MESH
PEERS = 15
HALO = tuple((dv, ds) for dv in (-1, 0, 1) for ds in (-1, 0, 1) if (dv, ds) != (0, 0))
UNROLL = 3
SCALE = 32 ** (-0.5)


def one_hot_rows(row):
    cell = lax.broadcasted_iota(jnp.int32, (256, 64), 0)
    return (cell == row).astype(F32).astype(BF)


def two(a, b):
    return jnp.concatenate([a.astype(F32), b.astype(F32)], axis=0).astype(BF)


def kernel(
    off_ref, src_ref, bc_ref, idx_ref, w_ref, gain_ref,
    global_hbm, cmap_hbm, state_hbm, cot_hbm, wqkv_hbm, wout_hbm, bias_hbm,
    update_ref, rgrad_ref, ggrad_ref,
    global_ref, cmap_ref, state_ref, cot_ref, wqkv_ref, wout_ref, bias_ref,
    asked, fetched, outbox, proj, bt, amat, at_ref, keep_ref, filled_ref,
    sidebox, cornerbox, patchbox, frow, fside, fcorner, crow, cside, ccorner, pside, prow,
    fext, cext, normed, cotw, qkv, gctx, ctx, gqkv, upd, gx, gfb, gfetch, landed, summed,
    load, req_send, req_recv, row_send, row_recv, halo_send, halo_recv, patch_send, patch_recv, back_send, back_recv,
):
    band, me = lax.axis_index("band"), lax.axis_index("tile")
    oy, ox = off_ref[0], off_ref[1]
    has = (band > 0, band < 7, me > 0, me < 15)
    edge = (band == 0) | (band == 7)
    side = (me == 0) | (me == 15)
    asks = edge | side
    gain = gain_ref[...]

    loads = [
        pltpu.make_async_copy(src, dst, load.at[n])
        for n, (src, dst) in enumerate((
            (state_hbm, state_ref), (cot_hbm, cot_ref), (global_hbm, global_ref), (cmap_hbm, cmap_ref),
            (wout_hbm, wout_ref), (wqkv_hbm, wqkv_ref), (bias_hbm, bias_ref),
        ))
    ]
    for one in loads:
        one.start()

    def place(dv, ds):
        return (lax.rem(band + 8 + dv, 8), lax.rem(me + 16 + ds, 16))

    def exists(dv, ds):
        ok = True
        if dv:
            ok = ok & (has[0] if dv < 0 else has[1])
        if ds:
            ok = ok & (has[2] if ds < 0 else has[3])
        return ok

    def other(n):
        return me ^ lax.rem(n * 7, 16)

    def other_asks(n):
        o = other(n)
        return edge | (o == 0) | (o == 15)

    barrier = pltpu.get_barrier_semaphore()
    for n in range(1, PEERS + 1):
        pl.semaphore_signal(barrier, inc=1, device_id=(band, other(n)), device_id_type=MESH)
    count = PEERS
    for dv, ds in HALO:
        if dv:
            count = count + exists(dv, ds).astype(jnp.int32)

            @pl.when(exists(dv, ds))
            def _(dv=dv, ds=ds):
                pl.semaphore_signal(barrier, inc=1, device_id=place(dv, ds), device_id_type=MESH)
    pl.semaphore_wait(barrier, count)

    def request(n):
        return pltpu.make_async_remote_copy(
            src_ref=src_ref.at[other(n)], dst_ref=asked.at[me], send_sem=req_send.at[n], recv_sem=req_recv.at[n],
            device_id=(band, other(n)), device_id_type=MESH,
        )

    @pl.when(asks)
    def _():
        for n in range(1, PEERS + 1):
            request(n).start()
        asked[me] = src_ref[me]

    def halo(which, h, dv, ds):
        own = state_hbm if which == 0 else cot_hbm
        rows, sides, corners = ((frow, fside, fcorner), (crow, cside, ccorner))[which]
        v, s = (0 if dv == 1 else 1), (0 if ds == 1 else 1)
        if ds == 0:
            src, dst = (own.at[0:7], rows.at[v, 0:7]) if dv == -1 else (own.at[9:16], rows.at[v, 1:8])
        elif dv == 0:
            src, dst = sidebox.at[2 * which + s], sides.at[s]
        else:
            src, dst = cornerbox.at[4 * which + 2 * v + s], corners.at[2 * v + s]
        return pltpu.make_async_remote_copy(
            src_ref=src, dst_ref=dst, send_sem=halo_send.at[8 * which + h], recv_sem=halo_recv.at[8 * which + h],
            device_id=place(dv, ds), device_id_type=MESH,
        )

    def send_halos(which):
        own = state_ref if which == 0 else cot_ref
        for h, (dv, ds) in enumerate(HALO):
            if ds == 0:
                @pl.when(exists(dv, ds))
                def _(h=h, dv=dv, ds=ds):
                    halo(which, h, dv, ds).start()
        loads[which].wait()
        for s in range(2):
            cols = slice(24, 32) if s == 0 else slice(0, 8)

            for y in range(8):
                sidebox[2 * which + s, y] = two(own[y][cols], own[y + 8][cols])
            for v in range(2):
                top = 8 if v == 0 else 0

                for y in range(4):
                    cornerbox[4 * which + 2 * v + s, y] = two(own[top + y][cols], own[top + y + 4][cols])
        for h, (dv, ds) in enumerate(HALO):
            if ds != 0:
                @pl.when(exists(dv, ds))
                def _(h=h, dv=dv, ds=ds):
                    halo(which, h, dv, ds).start()

    def halo_arrived(which):
        for h, (dv, ds) in enumerate(HALO):
            @pl.when(exists(-dv, -ds))
            def _(h=h, dv=dv, ds=ds):
                halo(which, h, dv, ds).wait_recv()

    def halo_sent(which):
        for h, (dv, ds) in enumerate(HALO):
            @pl.when(exists(dv, ds))
            def _(h=h, dv=dv, ds=ds):
                halo(which, h, dv, ds).wait_send()

    send_halos(0)
    send_halos(1)

    loads[2].wait()
    loads[3].wait()
    for n in range(2):
        cols = slice(256 * n, 256 * n + 256)
        proj[:, cols] = dot(global_ref[...], cmap_ref[:, cols]).astype(BF)

    def send_row(n):
        return pltpu.make_async_remote_copy(
            src_ref=outbox.at[other(n)], dst_ref=fetched.at[me], send_sem=row_send.at[n], recv_sem=row_recv.at[n],
            device_id=(band, other(n)), device_id_type=MESH,
        )

    @pl.loop(1, PEERS + 1)
    def _(n):
        @pl.when(other_asks(n))
        def _():
            request(n).wait_recv()
            hot = one_hot_rows(asked[other(n)])
            outbox[other(n)] = dot(hot, proj[...], ((0,), (0,))).astype(BF)
            send_row(n).start()

    @pl.when(asks)
    def _():
        fetched[me] = dot(one_hot_rows(asked[me]), proj[...], ((0,), (0,))).astype(BF)
        cell = lax.broadcasted_iota(jnp.int32, (512, 320), 0)
        hit = cell == bc_ref[...]
        relax = jnp.sum(w_ref[...], axis=0, keepdims=True)
        spread = jnp.sum(jnp.where(hit, relax, 0.0), axis=1, keepdims=True)
        keep_ref[...] = jnp.broadcast_to(1.0 - spread, (512, 128))
        hit = hit.astype(F32).astype(BF)

        def taps(m, carry):
            at = pl.ds(pl.multiple_of(m * 128, 128), 128)
            f = lax.broadcasted_iota(jnp.int32, (128, 320), 0) + m * 128
            total = jnp.zeros((128, 320), F32)
            for k in range(4):
                total = total + jnp.where(idx_ref[k : k + 1, :] == f, w_ref[k : k + 1, :], 0.0)
            bt[at, :] = total.astype(BF)
            at_ref[at, :] = dot(total.astype(BF), hit, ((1,), (1,))).astype(BF)
            return carry

        lax.fori_loop(0, 8, taps, 0)
        for m in range(4):
            at = slice(256 * m, 256 * m + 256)
            amat[:, at] = dot(hit, bt[at, :], ((1,), (1,))).astype(BF)

    @pl.when(jnp.logical_not(asks))
    def _():
        keep_ref[...] = jnp.ones((512, 128), F32)

    def clean(x, ok):
        return jnp.where(ok, x.astype(F32), 0.0)

    def spot(s):
        return slice(40, 48) if s == 0 else slice(32, 40)

    def build_own(ext, own):
        @pl.loop(0, 16, unroll=4)
        def _(y):
            ext[8 + y, 0:32] = own[y].astype(F32)

    def build_halo(ext, row, sides, corner):
        @pl.loop(0, 7)
        def _(y):
            ext[1 + y, 0:32] = clean(row[0, 1 + y], has[0])
            ext[24 + y, 0:32] = clean(row[1, y], has[1])

        @pl.loop(0, 8)
        def _(y):
            for s in range(2):
                both = clean(sides[s, y], has[2 + s])
                ext[8 + y, spot(s)] = both[0:8]
                ext[16 + y, spot(s)] = both[8:16]

        @pl.loop(0, 4)
        def _(y):
            for v in range(2):
                for s in range(2):
                    both = clean(corner[2 * v + s, y], has[v] & has[2 + s])
                    ext[24 * v + y, spot(s)] = both[0:8]
                    ext[24 * v + 4 + y, spot(s)] = both[8:16]

    def to_windows(src, dst, wy, norm):
        for p in range(4):
            base = pl.multiple_of(wy * STRIP + p * 16, 16)
            r = oy + wy * 8 + p * 2
            rows = []
            for q in range(2):
                x = pltpu.roll(src[r + q], 8 - ox, 0)[0:40]
                if norm:
                    x = norm_rows(x)[0] * gain
                rows.append(x)
            for wx in range(WX):
                piece = jnp.concatenate([rows[0][8 * wx : 8 * wx + 8], rows[1][8 * wx : 8 * wx + 8]], axis=0)
                dst[pl.ds(pl.multiple_of(base + wx * 64, 16), 16), :] = piece.astype(BF)

    def project(first, windows):
        cells = pl.ds(pl.multiple_of(first * 64, 64), windows * 64)
        x = normed[cells, :]
        for n in range(6):
            cols = slice(256 * n, 256 * n + 256)
            qkv[cells, cols] = dot(x, wqkv_ref[:, cols]).astype(BF)

    def attend(pick, first, last):
        @pl.loop(first, last)
        def _(turn):
            items = []
            for u in range(UNROLL):
                wy, wx = pick(turn * UNROLL + u)
                cells = pl.ds(pl.multiple_of((wy * WX + wx) * 64, 64), 64)
                j = lax.broadcasted_iota(jnp.int32, (64, 1), 0)
                ry = band * 16 + oy - 8 + wy * 8 + j // 8
                rx = me * 32 + ox - 8 + wx * 8 + j % 8
                inside = (ry >= 0) & (ry < 128) & (rx >= 0) & (rx < 512)
                shut = jnp.where(inside, 0.0, -1e30)
                for g in range(GROUPS):
                    items.append((cells, shut, g, 128 * g))
            qs = [qkv[c, lo : lo + 128] for c, _, _, lo in items]
            ks = [qkv[c, 512 + lo : 512 + lo + 128] for c, _, _, lo in items]
            vs = [qkv[c, 1024 + lo : 1024 + lo + 128] for c, _, _, lo in items]
            qbs = [block_diagonal(q) for q in qs]
            gbs = [block_diagonal(gctx[c, lo : lo + 128]) for c, _, _, lo in items]
            ss = [dot(k, qb, ((1,), (1,))) for k, qb in zip(ks, qbs)]
            gps = [dot(v, gb, ((1,), (1,))) for v, gb in zip(vs, gbs)]
            pbs, gls = [], []
            for s, gp, (_, shut, g, _) in zip(ss, gps, items):
                s = s * SCALE + (bias_ref[g] + shut)
                e = jnp.exp(s - jnp.max(s, axis=0, keepdims=True))
                p = e * (1.0 / jnp.sum(e, axis=0, keepdims=True))
                gs = p * (gp - jnp.sum(p * gp, axis=0, keepdims=True))
                pbs.append(p.astype(BF))
                gls.append((gs * SCALE).astype(BF))
            a = [dot(pb, v, ((0,), (0,))) for pb, v in zip(pbs, vs)]
            b = [dot(gl, k, ((0,), (0,))) for gl, k in zip(gls, ks)]
            c = [dot(gl, qb) for gl, qb in zip(gls, qbs)]
            d = [dot(pb, gb) for pb, gb in zip(pbs, gbs)]
            for n, (cells, _, _, lo) in enumerate(items):
                ctx[cells, lo : lo + 128] = diagonal_blocks(a[n]).astype(BF)
                gqkv[cells, lo : lo + 128] = diagonal_blocks(b[n]).astype(BF)
                gqkv[cells, 512 + lo : 512 + lo + 128] = c[n].astype(BF)
                gqkv[cells, 1024 + lo : 1024 + lo + 128] = d[n].astype(BF)

    build_own(cext, cot_ref)
    build_own(fext, state_ref)
    loads[4].wait()
    loads[5].wait()
    loads[6].wait()
    halo_arrived(0)
    build_halo(fext, frow, fside, fcorner)
    halo_arrived(1)
    build_halo(cext, crow, cside, ccorner)

    @pl.loop(0, WY)
    def _(wy):
        to_windows(cext, cotw, wy, False)
        cells = pl.ds(pl.multiple_of(wy * STRIP, 64), STRIP)
        for n in range(2):
            cols = slice(256 * n, 256 * n + 256)
            gctx[cells, cols] = dot(cotw[cells, :], wout_ref[cols, :], ((1,), (1,))).astype(BF)

    early = 2 * (1 - band // 4)
    start = 2 * (1 - me // 8)
    rest = 3 * (me // 8)
    to_windows(fext, normed, early, True)
    project(early * WX + start, 3)
    attend(lambda n: (early, start + n), 0, 1)

    @pl.when(asks)
    def _():
        @pl.loop(1, PEERS + 1)
        def _(n):
            send_row(n).wait_recv()

        for n in range(2):
            cols = slice(256 * n, 256 * n + 256)
            rows = jnp.concatenate([fetched[o, :, cols] for o in range(16)], axis=0)
            for y in range(4):
                at = slice(128 * y, 128 * y + 128)
                own = state_ref[4 * y : 4 * y + 4, :, cols].reshape(128, 256).astype(F32)
                x = own * keep_ref[at, 0:1] + dot(amat[at, :], rows)
                filled_ref[4 * y : 4 * y + 4, :, cols] = x.astype(BF).reshape(4, 32, 256)

    @pl.when(jnp.logical_not(asks))
    def _():
        filled_ref[...] = state_ref[...]

    def patch(n):
        s = n % 2
        if n < 2:
            dst, to = pside.at[s], place(0, 1 if s == 0 else -1)
        else:
            dst, to = prow.at[s], place(1 if s == 0 else -1, 0)
        return pltpu.make_async_remote_copy(
            src_ref=patchbox.at[n], dst_ref=dst, send_sem=patch_send.at[n], recv_sem=patch_recv.at[n],
            device_id=to, device_id_type=MESH,
        )

    PATCH = ((0, 1), (0, -1), (1, 0), (-1, 0))

    def patches(top, left, first):
        for s in range(2):
            if first == 0:
                y0, x0 = top, (24 if s == 0 else 0)
            else:
                y0, x0 = (8 if s == 0 else 0), left

            @pl.when(exists(*PATCH[first + s]))
            def _(n=first + s, y0=y0, x0=x0):
                for y in range(4):
                    patchbox[n, y] = two(filled_ref[y0 + y][x0 : x0 + 8], filled_ref[y0 + y + 4][x0 : x0 + 8])
                patch(n).start()

    for here, top in ((band == 0, 0), (band == 7, 8)):
        @pl.when(here)
        def _(top=top):
            patches(top, 0, 0)

    for here, left in ((me == 0, 0), (me == 15, 24)):
        @pl.when(here)
        def _(left=left):
            patches(0, left, 2)

    @pl.when(asks)
    def _():
        build_own(fext, filled_ref)

    for s in range(2):
        for here, top in ((band == 0, 0), (band == 7, 8)):
            @pl.when(here & has[2 + s])
            def _(s=s, top=top):
                patch(s).wait_recv()
                for y in range(4):
                    both = pside[s, y].astype(F32)
                    fext[8 + top + y, spot(s)] = both[0:8]
                    fext[12 + top + y, spot(s)] = both[8:16]
        for here, left in ((me == 0, 0), (me == 15, 24)):
            @pl.when(here & has[s])
            def _(s=s, left=left):
                patch(2 + s).wait_recv()
                for y in range(4):
                    both = prow[s, y].astype(F32)
                    fext[24 * s + y, left : left + 8] = both[0:8]
                    fext[24 * s + 4 + y, left : left + 8] = both[8:16]

    first = 1 - early // 2

    @pl.loop(0, 2)
    def _(n):
        to_windows(fext, normed, first + n, True)
        project((first + n) * WX, WX)

    to_windows(fext, normed, early, True)
    project(early * WX + rest, 2)

    def late(n):
        last = n // 10
        wy = (1 - last) * (first + n // WX) + last * early
        wx = (1 - last) * lax.rem(n, WX) + last * (rest + n - 10)
        return wy, wx

    attend(late, 0, 4)

    def scatter(dst, wy, cols, x):
        for wx in range(WX):
            for iy in range(8):
                at = 64 * wx + 8 * iy
                dst[8 * wy + iy, 8 * wx : 8 * wx + 8, cols] = x[at : at + 8]

    @pl.loop(0, WY)
    def _(wy):
        cells = pl.ds(pl.multiple_of(wy * STRIP, 64), STRIP)
        for n in range(2):
            cols = slice(256 * n, 256 * n + 256)
            scatter(gx, wy, cols, dot(gqkv[cells, :], wqkv_ref[cols, :], ((1,), (1,))))

    @pl.loop(0, 16, unroll=4)
    def _(y):
        p = pltpu.roll(gx[y + 8 - oy], 32 + ox, 0)[0:32] * gain
        normal, inverse = norm_rows(filled_ref[y].astype(F32))
        g = inverse * (
            p - jnp.mean(p, axis=-1, keepdims=True) - normal * jnp.mean(p * normal, axis=-1, keepdims=True)
        )
        at = pl.ds(pl.multiple_of(y * 32, 32), 32)
        rgrad_ref[y] = (g * keep_ref[at, 0:1]).astype(BF)
        gfb[at, :] = g.astype(BF)

    def send_back(n):
        return pltpu.make_async_remote_copy(
            src_ref=gfetch.at[other(n)], dst_ref=landed.at[me], send_sem=back_send.at[n], recv_sem=back_recv.at[n],
            device_id=(band, other(n)), device_id_type=MESH,
        )

    @pl.when(asks)
    def _():
        for m in range(4):
            at = slice(256 * m, 256 * m + 256)
            for n in range(2):
                cols = slice(256 * n, 256 * n + 256)
                g = dot(at_ref[at, :], gfb[:, cols]).astype(BF)
                for o in range(4):
                    gfetch[4 * m + o, :, cols] = g[64 * o : 64 * o + 64]

        @pl.loop(1, PEERS + 1)
        def _(n):
            send_back(n).start()

    @pl.loop(0, WY)
    def _(wy):
        cells = pl.ds(pl.multiple_of(wy * STRIP, 64), STRIP)
        for n in range(2):
            cols = slice(256 * n, 256 * n + 256)
            scatter(upd, wy, cols, dot(ctx[cells, :], wout_ref[:, cols]))

    @pl.loop(0, 16, unroll=4)
    def _(y):
        update_ref[y] = pltpu.roll(upd[y + 8 - oy], 32 + ox, 0)[0:32].astype(BF)

    summed[...] = jnp.zeros((256, C), F32)

    @pl.when(asks)
    def _():
        summed[...] = dot(one_hot_rows(asked[me]), gfetch[me])

    @pl.loop(1, PEERS + 1)
    def _(n):
        @pl.when(other_asks(n))
        def _():
            send_back(n).wait_recv()
            summed[...] += dot(one_hot_rows(asked[other(n)]), landed[other(n)])

    total = summed[...]
    high = total.astype(BF)
    low = (total - high.astype(F32)).astype(BF)
    for n in range(4):
        at = slice(256 * n, 256 * n + 256)
        m = cmap_ref[at, :]
        ggrad_ref[:, at] = (dot(high, m, ((1,), (1,))) + dot(low, m, ((1,), (1,)))).astype(BF)

    halo_sent(0)
    halo_sent(1)

    @pl.when(asks)
    def _():
        @pl.loop(1, PEERS + 1)
        def _(n):
            request(n).wait_send()
            send_back(n).wait_send()

    @pl.loop(1, PEERS + 1)
    def _(n):
        @pl.when(other_asks(n))
        def _():
            send_row(n).wait_send()

    for here, base in ((edge, 0), (side, 2)):
        for s in range(2):
            @pl.when(here & exists(*PATCH[base + s]))
            def _(n=base + s):
                patch(n).wait_send()


def shards(
    regional_state, global_state, boundary_cells, source_rows, interp_index, interp_weights, window_offsets,
    ln_gain, channel_map_weight, qkv_weight, out_weight, pos_bias, update_cot,
):
    idx = interp_index.reshape(320, 4).T
    w = interp_weights.reshape(320, 4).T
    bias = pos_bias.reshape(4, 4, 64, 64).transpose(0, 3, 1, 2).reshape(4, 64, 256)
    vm = pl.BlockSpec(memory_space=pltpu.VMEM)
    hbm = pl.BlockSpec(memory_space=pl.ANY)
    smem = pl.BlockSpec(memory_space=pltpu.SMEM)
    v = pltpu.VMEM
    sems = pltpu.SemaphoreType.DMA
    update, rgrad, ggrad = pl.pallas_call(
        kernel,
        out_shape=(
            jax.ShapeDtypeStruct((16, 32, C), BF),
            jax.ShapeDtypeStruct((16, 32, C), BF),
            jax.ShapeDtypeStruct((256, 1024), BF),
        ),
        in_specs=[smem] + [vm] * 5 + [hbm] * 7,
        out_specs=(vm, vm, vm),
        scratch_shapes=[
            v((256, 1024), BF), v((1024, C), BF), v((16, 32, C), BF), v((16, 32, C), BF),
            v((C, 3 * C), BF), v((C, C), BF), v((4, 64, 256), F32),
            v((16, 1, 64), jnp.int32), v((16, 64, C), BF), v((16, 64, C), BF), v((256, C), BF),
            v((1024, 320), BF), v((512, 1024), BF), v((1024, 512), BF), v((512, 128), F32), v((16, 32, C), BF),
            v((4, 8, 16, C), BF), v((8, 4, 16, C), BF), v((4, 4, 16, C), BF),
            v((2, 8, 32, C), BF), v((2, 8, 16, C), BF), v((4, 4, 16, C), BF),
            v((2, 8, 32, C), BF), v((2, 8, 16, C), BF), v((4, 4, 16, C), BF),
            v((2, 4, 16, C), BF), v((2, 4, 16, C), BF),
            v((32, 48, C), F32), v((32, 48, C), F32), v((960, C), BF), v((960, C), BF), v((960, 3 * C), BF),
            v((960, C), BF), v((960, C), BF), v((960, 3 * C), BF), v((24, 40, C), F32), v((24, 40, C), F32),
            v((512, C), BF), v((16, 64, C), BF), v((16, 64, C), BF), v((256, C), F32),
            sems((7,)), sems((16,)), sems((16,)), sems((16,)), sems((16,)), sems((16,)), sems((16,)),
            sems((4,)), sems((4,)), sems((16,)), sems((16,)),
        ],
        compiler_params=pltpu.CompilerParams(
            collective_id=0, has_side_effects=True, vmem_limit_bytes=60 * 2**20
        ),
        cost_estimate=pl.CostEstimate(flops=8 * 10**9, bytes_accessed=8 * 10**6, transcendentals=10**6),
    )(
        window_offsets, source_rows.reshape(16, 1, 64), boundary_cells.reshape(1, 320), idx, w, ln_gain.reshape(1, C),
        global_state.reshape(256, 1024), channel_map_weight, regional_state, update_cot, qkv_weight, out_weight, bias,
    )
    return update, rgrad, ggrad.reshape(16, 16, 1024)


def solution(mesh):
    tiled = P("band", "tile", None)
    deep = P("band", "tile", None, None)
    return jax.shard_map(
        shards,
        mesh=mesh,
        in_specs=(tiled, tiled, tiled, deep, deep, deep, P(), P(), P(), P(), P(), P(), tiled),
        out_specs=(tiled, tiled, tiled),
        check_vma=False,
    )
```

```python
import functools

import jax
import jax.numpy as jnp
from jax import lax
from jax.experimental import pallas as pl
from jax.experimental.pallas import tpu as pltpu
from jax.sharding import PartitionSpec as P

WS = 8
C = 512
HEADS = 16
GROUPS = 4
WY = 3
WX = 5
STRIP = WX * 64
EPS = 1e-05
BF = jnp.bfloat16
F32 = jnp.float32


def dot(a, b, dims=((1,), (0,))):
    return lax.dot_general(a, b, (dims, ((), ())), preferred_element_type=F32)


def norm_rows(x):
    centred = x - jnp.mean(x, axis=-1, keepdims=True)
    inverse = lax.rsqrt(jnp.mean(centred * centred, axis=-1, keepdims=True) + EPS)
    return centred * inverse, inverse


def block_diagonal(x):
    lane = lax.broadcasted_iota(jnp.int32, x.shape, 1) // 32
    return jnp.concatenate([jnp.where(lane == h, x, jnp.zeros_like(x)) for h in range(4)], axis=0)


def diagonal_blocks(x):
    lane = lax.broadcasted_iota(jnp.int32, (64, 128), 1) // 32
    out = x[192:256]
    for h in (2, 1, 0):
        out = jnp.where(lane == h, x[64 * h : 64 * h + 64], out)
    return out


MESH = pl.DeviceIdType.MESH
PEERS = 15
HALO = ((-1, 0), (1, 0), (0, -1), (0, 1), (0, -1), (0, 1), (0, -1), (0, 1))
UNROLL = 3
SCALE = 32 ** (-0.5)


def one_hot_rows(row):
    cell = lax.broadcasted_iota(jnp.int32, (256, row.shape[-1]), 0)
    return (cell == row).astype(F32).astype(BF)


def two(a, b):
    return jnp.concatenate([a.astype(F32), b.astype(F32)], axis=0).astype(BF)


def kernel(
    off_ref, src_ref, bc_ref, idx_ref, w_ref, gain_ref,
    global_hbm, cmap_hbm, state_hbm, cot_hbm, wqkv_hbm, wout_hbm, raw_hbm,
    update_ref, rgrad_ref, ggrad_ref,
    global_ref, cmap_ref, state_ref, cot_ref, wqkv_ref, wout_ref, raw_ref, lined, bias_ref,
    asked, fetched, outbox, proj, bt, amat, at_ref, keep_ref, filled_ref,
    sidebox, cornerbox, patchbox, frow, fside, fcorner, crow, cside, ccorner, pside, prow,
    fext, cext, normed, cotw, qkv, gctx, ctx, gqkv, upd, gx, gfb, gfetch, landed, summed,
    load, req_send, req_recv, row_send, row_recv, halo_send, halo_recv, patch_send, patch_recv, back_send, back_recv,
):
    band, me = lax.axis_index("band"), lax.axis_index("tile")
    oy, ox = off_ref[0], off_ref[1]
    has = (band > 0, band < 7, me > 0, me < 15)
    edge = (band == 0) | (band == 7)
    side = (me == 0) | (me == 15)
    asks = edge | side
    gain = gain_ref[...]

    loads = [
        pltpu.make_async_copy(src, dst, load.at[n])
        for n, (src, dst) in enumerate((
            (state_hbm, state_ref), (cot_hbm, cot_ref), (global_hbm, global_ref), (cmap_hbm, cmap_ref),
            (wout_hbm, wout_ref), (wqkv_hbm, wqkv_ref), (raw_hbm, raw_ref),
        ))
    ]
    for n in (6, 0, 1, 2, 3, 4, 5):
        loads[n].start()

    def place(dv, ds):
        return (lax.rem(band + 8 + dv, 8), lax.rem(me + 16 + ds, 16))

    def exists(dv, ds):
        ok = True
        if dv:
            ok = ok & (has[0] if dv < 0 else has[1])
        if ds:
            ok = ok & (has[2] if ds < 0 else has[3])
        return ok

    def other(n):
        return me ^ lax.rem(n * 7, 16)

    def other_asks(n):
        o = other(n)
        return edge | (o == 0) | (o == 15)

    barrier = pltpu.get_barrier_semaphore()
    for n in range(1, PEERS + 1):
        pl.semaphore_signal(barrier, inc=1, device_id=(band, other(n)), device_id_type=MESH)
    count = PEERS
    for dv, ds in HALO[0:2]:
        if dv:
            count = count + exists(dv, ds).astype(jnp.int32)

            @pl.when(exists(dv, ds))
            def _(dv=dv, ds=ds):
                pl.semaphore_signal(barrier, inc=1, device_id=place(dv, ds), device_id_type=MESH)
    loads[6].wait()
    for i in range(64):
        lined[:, i, :] = raw_ref[:, 64 * i : 64 * i + 64]
    for g in range(GROUPS):
        bias_ref[g] = lined[4 * g : 4 * g + 4].reshape(256, 64).T
    pl.semaphore_wait(barrier, count)

    def request(n):
        return pltpu.make_async_remote_copy(
            src_ref=src_ref.at[other(n)], dst_ref=asked.at[me], send_sem=req_send.at[n], recv_sem=req_recv.at[n],
            device_id=(band, other(n)), device_id_type=MESH,
        )

    @pl.when(asks)
    def _():
        for n in range(1, PEERS + 1):
            request(n).start()
        asked[me] = src_ref[me]

    def halo(which, h):
        own = state_hbm if which == 0 else cot_hbm
        rows, sides, corners = ((frow, fside, fcorner), (crow, cside, ccorner))[which]
        src, dst = (
            (own.at[0:7], rows.at[1, 0:7]),
            (own.at[9:16], rows.at[0, 1:8]),
            (sidebox.at[2 * which + 1], sides.at[1]),
            (sidebox.at[2 * which], sides.at[0]),
            (cornerbox.at[2 * which + 1], corners.at[1]),
            (cornerbox.at[2 * which], corners.at[0]),
            (cornerbox.at[2 * which + 1, 0:4], corners.at[1, 0:4]),
            (cornerbox.at[2 * which, 0:4], corners.at[0, 0:4]),
        )[h]
        return pltpu.make_async_remote_copy(
            src_ref=src, dst_ref=dst, send_sem=halo_send.at[8 * which + h], recv_sem=halo_recv.at[8 * which + h],
            device_id=place(*HALO[h]), device_id_type=MESH,
        )

    def clean(x, ok):
        return jnp.where(ok, x.astype(F32), 0.0)

    def used(h):
        return True if h < 4 else jnp.logical_not(edge) if h < 6 else edge

    def send_halo(which, hs):
        for h in hs:
            @pl.when(exists(*HALO[h]) & used(h))
            def _(h=h):
                halo(which, h).start()

    def halo_arrived(which, hs):
        for h in hs:
            @pl.when(exists(-HALO[h][0], -HALO[h][1]) & used(h))
            def _(h=h):
                halo(which, h).wait_recv()

    def halo_sent(which):
        for h in range(8):
            @pl.when(exists(*HALO[h]) & used(h))
            def _(h=h):
                halo(which, h).wait_send()

    def send_sides(which):
        own = state_ref if which == 0 else cot_ref
        loads[which].wait()
        for s in range(2):
            cols = slice(24, 32) if s == 0 else slice(0, 8)
            for y in range(8):
                sidebox[2 * which + s, y] = two(own[y][cols], own[y + 8][cols])
        send_halo(which, (2, 3))

    def send_corners(which):
        rows = frow if which == 0 else crow
        halo_arrived(which, (0, 1))
        for s in range(2):
            cols = slice(24, 32) if s == 0 else slice(0, 8)

            @pl.when(jnp.logical_not(edge))
            def _(s=s, cols=cols):
                for y in range(7):
                    cornerbox[2 * which + s, y] = two(rows[0, 1 + y][cols], rows[1, y][cols])

            for here, v in ((band == 7, 0), (band == 0, 1)):
                @pl.when(here)
                def _(s=s, cols=cols, v=v):
                    for y in range(4):
                        low = rows[v, y][cols] if v == 1 or y else jnp.zeros((8, C), BF)
                        high = rows[v, y + 4][cols] if v == 0 or y < 3 else jnp.zeros((8, C), BF)
                        cornerbox[2 * which + s, y] = two(low, high)
        send_halo(which, (4, 5, 6, 7))

    send_halo(0, (0, 1))
    send_halo(1, (0, 1))

    @pl.when(edge)
    def _():
        send_sides(0)
        send_sides(1)

    loads[2].wait()
    loads[3].wait()
    for n in range(2):
        cols = slice(256 * n, 256 * n + 256)
        proj[:, cols] = dot(global_ref[...], cmap_ref[:, cols]).astype(BF)

    def send_row(n):
        return pltpu.make_async_remote_copy(
            src_ref=outbox.at[other(n)], dst_ref=fetched.at[me], send_sem=row_send.at[n], recv_sem=row_recv.at[n],
            device_id=(band, other(n)), device_id_type=MESH,
        )

    @pl.when(edge)
    def _():
        @pl.loop(0, 5)
        def _(t):
            group = [1 + 3 * t + u for u in range(3)]
            for n in group:
                request(n).wait_recv()
            hot = one_hot_rows(jnp.concatenate([asked[other(n)] for n in group], axis=1))
            rows = dot(hot, proj[...], ((0,), (0,))).astype(BF)
            for u, n in enumerate(group):
                outbox[other(n)] = rows[64 * u : 64 * u + 64]
                send_row(n).start()

    @pl.loop(1, PEERS + 1)
    def _(n):
        @pl.when(other_asks(n) & jnp.logical_not(edge))
        def _():
            request(n).wait_recv()
            hot = one_hot_rows(asked[other(n)])
            outbox[other(n)] = dot(hot, proj[...], ((0,), (0,))).astype(BF)
            send_row(n).start()

    @pl.when(jnp.logical_not(edge))
    def _():
        send_sides(0)
        send_sides(1)

    @pl.when(asks)
    def _():
        fetched[me] = dot(one_hot_rows(asked[me]), proj[...], ((0,), (0,))).astype(BF)
        cell = lax.broadcasted_iota(jnp.int32, (512, 320), 0)
        hit = cell == bc_ref[...]
        relax = jnp.sum(w_ref[...], axis=0, keepdims=True)
        spread = jnp.sum(jnp.where(hit, relax, 0.0), axis=1, keepdims=True)
        keep_ref[...] = jnp.broadcast_to(1.0 - spread, (512, 128))
        hit = hit.astype(F32).astype(BF)

        def taps(m, carry):
            at = pl.ds(pl.multiple_of(m * 128, 128), 128)
            f = lax.broadcasted_iota(jnp.int32, (128, 320), 0) + m * 128
            total = jnp.zeros((128, 320), F32)
            for k in range(4):
                total = total + jnp.where(idx_ref[k : k + 1, :] == f, w_ref[k : k + 1, :], 0.0)
            bt[at, :] = total.astype(BF)
            return carry

        lax.fori_loop(0, 8, taps, 0)
        for m in range(2):
            at = slice(512 * m, 512 * m + 512)
            at_ref[at, :] = dot(bt[at, :], hit, ((1,), (1,))).astype(BF)
        for m in range(4):
            at = slice(256 * m, 256 * m + 256)
            amat[:, at] = dot(hit, bt[at, :], ((1,), (1,))).astype(BF)

    @pl.when(jnp.logical_not(asks))
    def _():
        keep_ref[...] = jnp.ones((512, 128), F32)

    def spot(s):
        return slice(40, 48) if s == 0 else slice(32, 40)

    def build_own(ext, own):
        @pl.loop(0, 16, unroll=4)
        def _(y):
            ext[8 + y, 0:32] = own[y].astype(F32)

    def build_halo(ext, row, sides, corner):
        @pl.loop(0, 7)
        def _(y):
            ext[1 + y, 0:32] = clean(row[0, 1 + y], has[0])
            ext[24 + y, 0:32] = clean(row[1, y], has[1])

        @pl.when(jnp.logical_not(edge))
        def _():
            @pl.loop(0, 7)
            def _(y):
                for s in range(2):
                    both = clean(corner[s, y], has[2 + s])
                    ext[1 + y, spot(s)] = both[0:8]
                    ext[24 + y, spot(s)] = both[8:16]

        for here, v in ((band == 7, 0), (band == 0, 1)):
            @pl.when(here)
            def _(v=v):
                @pl.loop(0, 4)
                def _(y):
                    for s in range(2):
                        both = clean(corner[s, y], has[2 + s])
                        ext[24 * v + y, spot(s)] = both[0:8]
                        ext[24 * v + 4 + y, spot(s)] = both[8:16]
                        ext[24 * (1 - v) + y, spot(s)] = jnp.zeros((8, C), F32)
                        ext[24 * (1 - v) + 4 + y, spot(s)] = jnp.zeros((8, C), F32)

        @pl.loop(0, 8)
        def _(y):
            for s in range(2):
                both = clean(sides[s, y], has[2 + s])
                ext[8 + y, spot(s)] = both[0:8]
                ext[16 + y, spot(s)] = both[8:16]

    def to_windows(src, dst, wy, norm):
        for p in range(4):
            base = pl.multiple_of(wy * STRIP + p * 16, 16)
            r = oy + wy * 8 + p * 2
            rows = []
            for q in range(2):
                x = pltpu.roll(src[r + q], 8 - ox, 0)[0:40]
                if norm:
                    x = norm_rows(x)[0] * gain
                rows.append(x)
            for wx in range(WX):
                piece = jnp.concatenate([rows[0][8 * wx : 8 * wx + 8], rows[1][8 * wx : 8 * wx + 8]], axis=0)
                dst[pl.ds(pl.multiple_of(base + wx * 64, 16), 16), :] = piece.astype(BF)

    def project(first, windows):
        cells = pl.ds(pl.multiple_of(first * 64, 64), windows * 64)
        x = normed[cells, :]
        for n in range(6):
            cols = slice(256 * n, 256 * n + 256)
            qkv[cells, cols] = dot(x, wqkv_ref[:, cols]).astype(BF)

    def attend(pick, first, last):
        @pl.loop(first, last)
        def _(turn):
            items = []
            for u in range(UNROLL):
                wy, wx = pick(turn * UNROLL + u)
                cells = pl.ds(pl.multiple_of((wy * WX + wx) * 64, 64), 64)
                j = lax.broadcasted_iota(jnp.int32, (64, 1), 0)
                ry = band * 16 + oy - 8 + wy * 8 + j // 8
                rx = me * 32 + ox - 8 + wx * 8 + j % 8
                inside = (ry >= 0) & (ry < 128) & (rx >= 0) & (rx < 512)
                shut = jnp.where(inside, 0.0, -1e30)
                for g in range(GROUPS):
                    items.append((cells, shut, g, 128 * g))
            qs = [qkv[c, lo : lo + 128] for c, _, _, lo in items]
            ks = [qkv[c, 512 + lo : 512 + lo + 128] for c, _, _, lo in items]
            vs = [qkv[c, 1024 + lo : 1024 + lo + 128] for c, _, _, lo in items]
            qbs = [block_diagonal(q) for q in qs]
            gbs = [block_diagonal(gctx[c, lo : lo + 128]) for c, _, _, lo in items]
            ss = [dot(k, qb, ((1,), (1,))) for k, qb in zip(ks, qbs)]
            gps = [dot(v, gb, ((1,), (1,))) for v, gb in zip(vs, gbs)]
            pbs, gls = [], []
            for s, gp, (_, shut, g, _) in zip(ss, gps, items):
                s = s * SCALE + (bias_ref[g] + shut)
                e = jnp.exp(s - jnp.max(s, axis=0, keepdims=True))
                p = e * (1.0 / jnp.sum(e, axis=0, keepdims=True))
                gs = p * (gp - jnp.sum(p * gp, axis=0, keepdims=True))
                pbs.append(p.astype(BF))
                gls.append((gs * SCALE).astype(BF))
            a = [dot(pb, v, ((0,), (0,))) for pb, v in zip(pbs, vs)]
            b = [dot(gl, k, ((0,), (0,))) for gl, k in zip(gls, ks)]
            c = [dot(gl, qb) for gl, qb in zip(gls, qbs)]
            d = [dot(pb, gb) for pb, gb in zip(pbs, gbs)]
            for n, (cells, _, _, lo) in enumerate(items):
                ctx[cells, lo : lo + 128] = diagonal_blocks(a[n]).astype(BF)
                gqkv[cells, lo : lo + 128] = diagonal_blocks(b[n]).astype(BF)
                gqkv[cells, 512 + lo : 512 + lo + 128] = c[n].astype(BF)
                gqkv[cells, 1024 + lo : 1024 + lo + 128] = d[n].astype(BF)

    build_own(cext, cot_ref)
    send_corners(0)
    send_corners(1)

    @pl.when(asks)
    def _():
        @pl.loop(1, PEERS + 1)
        def _(n):
            send_row(n).wait_recv()

        for n in range(2):
            cols = slice(256 * n, 256 * n + 256)
            rows = jnp.concatenate([fetched[o, :, cols] for o in range(16)], axis=0)
            for y in range(4):
                at = slice(128 * y, 128 * y + 128)
                own = state_ref[4 * y : 4 * y + 4, :, cols].reshape(128, 256).astype(F32)
                x = own * keep_ref[at, 0:1] + dot(amat[at, :], rows)
                filled_ref[4 * y : 4 * y + 4, :, cols] = x.astype(BF).reshape(4, 32, 256)

    @pl.when(jnp.logical_not(asks))
    def _():
        filled_ref[...] = state_ref[...]

    def patch(n):
        s = n % 2
        if n < 2:
            dst, to = pside.at[s], place(0, 1 if s == 0 else -1)
        else:
            dst, to = prow.at[s], place(1 if s == 0 else -1, 0)
        return pltpu.make_async_remote_copy(
            src_ref=patchbox.at[n], dst_ref=dst, send_sem=patch_send.at[n], recv_sem=patch_recv.at[n],
            device_id=to, device_id_type=MESH,
        )

    PATCH = ((0, 1), (0, -1), (1, 0), (-1, 0))

    def patches(top, left, first):
        for s in range(2):
            if first == 0:
                y0, x0 = top, (24 if s == 0 else 0)
            else:
                y0, x0 = (8 if s == 0 else 0), left

            @pl.when(exists(*PATCH[first + s]))
            def _(n=first + s, y0=y0, x0=x0):
                for y in range(4):
                    patchbox[n, y] = two(filled_ref[y0 + y][x0 : x0 + 8], filled_ref[y0 + y + 4][x0 : x0 + 8])
                patch(n).start()

    for here, top in ((band == 0, 0), (band == 7, 8)):
        @pl.when(here)
        def _(top=top):
            patches(top, 0, 0)

    for here, left in ((me == 0, 0), (me == 15, 24)):
        @pl.when(here)
        def _(left=left):
            patches(0, left, 2)

    build_own(fext, filled_ref)
    loads[4].wait()
    loads[5].wait()
    halo_arrived(0, (2, 3, 4, 5, 6, 7))
    build_halo(fext, frow, fside, fcorner)
    halo_arrived(1, (2, 3, 4, 5, 6, 7))
    build_halo(cext, crow, cside, ccorner)

    @pl.loop(0, WY)
    def _(wy):
        to_windows(cext, cotw, wy, False)
        cells = pl.ds(pl.multiple_of(wy * STRIP, 64), STRIP)
        for n in range(2):
            cols = slice(256 * n, 256 * n + 256)
            gctx[cells, cols] = dot(cotw[cells, :], wout_ref[cols, :], ((1,), (1,))).astype(BF)

    for s in range(2):
        for here, top in ((band == 0, 0), (band == 7, 8)):
            @pl.when(here & has[2 + s])
            def _(s=s, top=top):
                patch(s).wait_recv()
                for y in range(4):
                    both = pside[s, y].astype(F32)
                    fext[8 + top + y, spot(s)] = both[0:8]
                    fext[12 + top + y, spot(s)] = both[8:16]
        for here, left in ((me == 0, 0), (me == 15, 24)):
            @pl.when(here & has[s])
            def _(s=s, left=left):
                patch(2 + s).wait_recv()
                for y in range(4):
                    both = prow[s, y].astype(F32)
                    fext[24 * s + y, left : left + 8] = both[0:8]
                    fext[24 * s + 4 + y, left : left + 8] = both[8:16]

    early = 2 * (1 - band // 4)
    start = 2 * (1 - me // 8)
    rest = 3 * (me // 8)
    first = 1 - early // 2

    @pl.loop(0, 2)
    def _(n):
        to_windows(fext, normed, first + n, True)
        project((first + n) * WX, WX)

    to_windows(fext, normed, early, True)
    project(early * WX + rest, 2)

    def late(n):
        last = n // 10
        wy = (1 - last) * (first + n // WX) + last * early
        wx = (1 - last) * lax.rem(n, WX) + last * (rest + n - 10)
        return wy, wx

    attend(late, 0, 4)

    def scatter(dst, wy, wx, windows, cols, x):
        for u in range(windows):
            for iy in range(8):
                at = 64 * u + 8 * iy
                dst[8 * wy + iy, pl.ds(pl.multiple_of(8 * (wx + u), 8), 8), cols] = x[at : at + 8]

    def input_gradient(wy, wx, windows):
        cells = pl.ds(pl.multiple_of((wy * WX + wx) * 64, 64), windows * 64)
        for n in range(2):
            cols = slice(256 * n, 256 * n + 256)
            scatter(gx, wy, wx, windows, cols, dot(gqkv[cells, :], wqkv_ref[cols, :], ((1,), (1,))))

    for iy in range(8):
        gx[8 * early + iy, pl.ds(pl.multiple_of(8 * start, 8), 24), :] = jnp.zeros((24, C), F32)

    @pl.loop(0, 2)
    def _(n):
        input_gradient(first + n, 0, WX)

    input_gradient(early, rest, 2)

    def norm_gradient(y):
        p = pltpu.roll(gx[y + 8 - oy], 32 + ox, 0)[0:32] * gain
        normal, inverse = norm_rows(filled_ref[y].astype(F32))
        g = inverse * (
            p - jnp.mean(p, axis=-1, keepdims=True) - normal * jnp.mean(p * normal, axis=-1, keepdims=True)
        )
        at = pl.ds(pl.multiple_of(y * 32, 32), 32)
        rgrad_ref[y] = (g * keep_ref[at, 0:1]).astype(BF)
        gfb[at, :] = g.astype(BF)

    pl.loop(0, 16, unroll=4)(norm_gradient)

    def send_back(n):
        return pltpu.make_async_remote_copy(
            src_ref=gfetch.at[other(n)], dst_ref=landed.at[me], send_sem=back_send.at[n], recv_sem=back_recv.at[n],
            device_id=(band, other(n)), device_id_type=MESH,
        )

    @pl.when(asks)
    def _():
        for m in range(4):
            at = slice(256 * m, 256 * m + 256)
            for n in range(2):
                cols = slice(256 * n, 256 * n + 256)
                g = dot(at_ref[at, :], gfb[:, cols]).astype(BF)
                for o in range(4):
                    gfetch[4 * m + o, :, cols] = g[64 * o : 64 * o + 64]

        @pl.loop(1, PEERS + 1)
        def _(n):
            send_back(n).start()

    project(early * WX + start, 3)
    attend(lambda n: (early, start + n), 0, 1)
    input_gradient(early, start, 3)

    @pl.loop(0, 8, unroll=4)
    def _(y):
        norm_gradient(y + 4 * early)

    @pl.loop(0, WY)
    def _(wy):
        cells = pl.ds(pl.multiple_of(wy * STRIP, 64), STRIP)
        for n in range(2):
            cols = slice(256 * n, 256 * n + 256)
            scatter(upd, wy, 0, WX, cols, dot(ctx[cells, :], wout_ref[:, cols]))

    @pl.loop(0, 16, unroll=4)
    def _(y):
        update_ref[y] = pltpu.roll(upd[y + 8 - oy], 32 + ox, 0)[0:32].astype(BF)

    summed[...] = jnp.zeros((256, C), F32)

    @pl.when(asks)
    def _():
        summed[...] = dot(one_hot_rows(asked[me]), gfetch[me])

    @pl.when(edge)
    def _():
        for t in range(3):
            group = [1 + 5 * t + u for u in range(5)]
            for n in group:
                send_back(n).wait_recv()
            hot = one_hot_rows(jnp.concatenate([asked[other(n)] for n in group], axis=1))
            for c in range(2):
                cols = slice(256 * c, 256 * c + 256)
                rows = jnp.concatenate([landed[other(n), :, cols] for n in group], axis=0)
                summed[:, cols] += dot(hot, rows)

    @pl.loop(1, PEERS + 1)
    def _(n):
        @pl.when(other_asks(n) & jnp.logical_not(edge))
        def _():
            send_back(n).wait_recv()
            summed[...] += dot(one_hot_rows(asked[other(n)]), landed[other(n)])

    total = summed[...]
    high = total.astype(BF)
    low = (total - high.astype(F32)).astype(BF)
    for n in range(4):
        at = slice(256 * n, 256 * n + 256)
        m = cmap_ref[at, :]
        ggrad_ref[:, at] = (dot(high, m, ((1,), (1,))) + dot(low, m, ((1,), (1,)))).astype(BF)

    halo_sent(0)
    halo_sent(1)

    @pl.when(asks)
    def _():
        @pl.loop(1, PEERS + 1)
        def _(n):
            request(n).wait_send()
            send_back(n).wait_send()

    @pl.loop(1, PEERS + 1)
    def _(n):
        @pl.when(other_asks(n))
        def _():
            send_row(n).wait_send()

    for here, base in ((edge, 0), (side, 2)):
        for s in range(2):
            @pl.when(here & exists(*PATCH[base + s]))
            def _(n=base + s):
                patch(n).wait_send()


def hand_over(*refs):
    for n in range(3):
        refs[3 + n][...] = refs[n][...]


def shards(
    regional_state, global_state, boundary_cells, source_rows, interp_index, interp_weights, window_offsets,
    ln_gain, channel_map_weight, qkv_weight, out_weight, pos_bias, update_cot,
):
    idx = interp_index.reshape(320, 4).T
    w = interp_weights.reshape(320, 4).T
    vm = pl.BlockSpec(memory_space=pltpu.VMEM)
    hbm = pl.BlockSpec(memory_space=pl.ANY)
    smem = pl.BlockSpec(memory_space=pltpu.SMEM)
    v = pltpu.VMEM
    sems = pltpu.SemaphoreType.DMA
    update, rgrad, ggrad = pl.pallas_call(
        kernel,
        out_shape=(
            jax.ShapeDtypeStruct((16, 32, C), BF),
            jax.ShapeDtypeStruct((16, 32, C), BF),
            jax.ShapeDtypeStruct((256, 1024), BF),
        ),
        in_specs=[smem] + [vm] * 5 + [hbm] * 7,
        out_specs=(vm, vm, vm),
        scratch_shapes=[
            v((256, 1024), BF), v((1024, C), BF), v((16, 32, C), BF), v((16, 32, C), BF),
            v((C, 3 * C), BF), v((C, C), BF), v((HEADS, 4096), F32), v((HEADS, 64, 64), F32), v((4, 64, 256), F32),
            v((16, 1, 64), jnp.int32), v((16, 64, C), BF), v((16, 64, C), BF), v((256, C), BF),
            v((1024, 320), BF), v((512, 1024), BF), v((1024, 512), BF), v((512, 128), F32), v((16, 32, C), BF),
            v((4, 8, 16, C), BF), v((4, 7, 16, C), BF), v((4, 4, 16, C), BF),
            v((2, 8, 32, C), BF), v((2, 8, 16, C), BF), v((2, 7, 16, C), BF),
            v((2, 8, 32, C), BF), v((2, 8, 16, C), BF), v((2, 7, 16, C), BF),
            v((2, 4, 16, C), BF), v((2, 4, 16, C), BF),
            v((32, 48, C), F32), v((32, 48, C), F32), v((960, C), BF), v((960, C), BF), v((960, 3 * C), BF),
            v((960, C), BF), v((960, C), BF), v((960, 3 * C), BF), v((24, 40, C), F32), v((24, 40, C), F32),
            v((512, C), BF), v((16, 64, C), BF), v((16, 64, C), BF), v((256, C), F32),
            sems((7,)), sems((16,)), sems((16,)), sems((16,)), sems((16,)), sems((16,)), sems((16,)),
            sems((4,)), sems((4,)), sems((16,)), sems((16,)),
        ],
        compiler_params=pltpu.CompilerParams(
            collective_id=0, has_side_effects=True, vmem_limit_bytes=60 * 2**20
        ),
        cost_estimate=pl.CostEstimate(flops=8 * 10**9, bytes_accessed=8 * 10**6, transcendentals=10**6),
    )(
        window_offsets, source_rows.reshape(16, 1, 64), boundary_cells.reshape(1, 320), idx, w, ln_gain.reshape(1, C),
        global_state.reshape(256, 1024), channel_map_weight, regional_state, update_cot, qkv_weight, out_weight, pos_bias,
    )
    update, rgrad, ggrad = pl.pallas_call(
        hand_over,
        out_shape=(
            jax.ShapeDtypeStruct((16, 32, C), BF),
            jax.ShapeDtypeStruct((16, 32, C), BF),
            jax.ShapeDtypeStruct((256, 1024), BF),
        ),
        in_specs=[vm] * 3,
        out_specs=(vm,) * 3,
    )(update, rgrad, ggrad)
    return update, rgrad, ggrad.reshape(16, 16, 1024)


def solution(mesh):
    tiled = P("band", "tile", None)
    deep = P("band", "tile", None, None)
    return jax.shard_map(
        shards,
        mesh=mesh,
        in_specs=(tiled, tiled, tiled, deep, deep, deep, P(), P(), P(), P(), P(), P(), tiled),
        out_specs=(tiled, tiled, tiled),
        check_vma=False,
    )
```

```python
import functools

import jax
import jax.numpy as jnp
from jax import lax
from jax.experimental import pallas as pl
from jax.experimental.pallas import tpu as pltpu
from jax.sharding import PartitionSpec as P

WS = 8
C = 512
HEADS = 16
GROUPS = 4
WY = 3
WX = 5
STRIP = WX * 64
EPS = 1e-05
BF = jnp.bfloat16
F32 = jnp.float32


def dot(a, b, dims=((1,), (0,))):
    return lax.dot_general(a, b, (dims, ((), ())), preferred_element_type=F32)


def norm_rows(x):
    centred = x - jnp.mean(x, axis=-1, keepdims=True)
    inverse = lax.rsqrt(jnp.mean(centred * centred, axis=-1, keepdims=True) + EPS)
    return centred * inverse, inverse


def block_diagonal(x):
    lane = lax.broadcasted_iota(jnp.int32, x.shape, 1) // 32
    return jnp.concatenate([jnp.where(lane == h, x, jnp.zeros_like(x)) for h in range(4)], axis=0)


def diagonal_blocks(x):
    lane = lax.broadcasted_iota(jnp.int32, (64, 128), 1) // 32
    out = x[192:256]
    for h in (2, 1, 0):
        out = jnp.where(lane == h, x[64 * h : 64 * h + 64], out)
    return out


MESH = pl.DeviceIdType.MESH
PEERS = 15
HALO = ((-1, 0), (1, 0), (0, -1), (0, 1), (0, -1), (0, 1), (0, -1), (0, 1))
UNROLL = 3
SCALE = 32 ** (-0.5)


def one_hot_rows(row):
    cell = lax.broadcasted_iota(jnp.int32, (256, row.shape[-1]), 0)
    return (cell == row).astype(F32).astype(BF)


def two(a, b):
    return jnp.concatenate([a.astype(F32), b.astype(F32)], axis=0).astype(BF)


def kernel(
    off_ref, src_ref, bc_ref, idx_ref, w_ref, gain_ref,
    global_hbm, cmap_hbm, state_hbm, cot_hbm, wqkv_hbm, wout_hbm, raw_hbm,
    update_hbm, rgrad_hbm, ggrad_hbm,
    update_ref, rgrad_ref, ggrad_ref,
    global_ref, cmap_ref, state_ref, cot_ref, wqkv_ref, wout_ref, raw_ref, lined, bias_ref,
    asked, fetched, outbox, proj, bt, amat, at_ref, keep_ref, filled_ref,
    sidebox, cornerbox, diagbox, patchbox, frow, fside, fcorner, crow, cside, ccorner, pside, prow,
    fext, cext, normed, cotw, qkv, gctx, ctx, gqkv, upd, gx, gfb, gfetch, landed, summed,
    load, store, req_send, req_recv, row_send, row_recv, halo_send, halo_recv, patch_send, patch_recv, back_send, back_recv,
):
    band, me = lax.axis_index("band"), lax.axis_index("tile")
    oy, ox = off_ref[0], off_ref[1]
    has = (band > 0, band < 7, me > 0, me < 15)
    edge = (band == 0) | (band == 7)
    side = (me == 0) | (me == 15)
    asks = edge | side
    beside = (band == 1) | (band == 6)
    outward = 2 * (band // 4) - 1
    gain = gain_ref[...]

    loads = [
        pltpu.make_async_copy(src, dst, load.at[n])
        for n, (src, dst) in enumerate((
            (state_hbm, state_ref), (cot_hbm, cot_ref), (global_hbm, global_ref), (cmap_hbm, cmap_ref),
            (wout_hbm, wout_ref), (wqkv_hbm, wqkv_ref), (raw_hbm, raw_ref),
        ))
    ]
    for one in loads:
        one.start()

    def place(dv, ds):
        return (lax.rem(band + 8 + dv, 8), lax.rem(me + 16 + ds, 16))

    def exists(dv, ds):
        ok = True
        if dv:
            ok = ok & (has[0] if dv < 0 else has[1])
        if ds:
            ok = ok & (has[2] if ds < 0 else has[3])
        return ok

    def other(n):
        return me ^ lax.rem(n * 7, 16)

    def other_asks(n):
        o = other(n)
        return edge | (o == 0) | (o == 15)

    barrier = pltpu.get_barrier_semaphore()
    for n in range(1, PEERS + 1):
        pl.semaphore_signal(barrier, inc=1, device_id=(band, other(n)), device_id_type=MESH)
    count = PEERS
    for dv, ds in HALO[0:2]:
        if dv:
            count = count + exists(dv, ds).astype(jnp.int32)

            @pl.when(exists(dv, ds))
            def _(dv=dv, ds=ds):
                pl.semaphore_signal(barrier, inc=1, device_id=place(dv, ds), device_id_type=MESH)
    for dv, here in ((1, (band == 0) | (band == 6)), (-1, (band == 1) | (band == 7))):
        for ds in (-1, 1):
            count = count + (here & exists(0, ds)).astype(jnp.int32)

            @pl.when(here & exists(0, ds))
            def _(dv=dv, ds=ds):
                pl.semaphore_signal(barrier, inc=1, device_id=place(dv, ds), device_id_type=MESH)
    for which, own in ((0, state_ref), (1, cot_ref)):
        loads[which].wait()
        for s in range(2):
            cols = slice(24, 32) if s == 0 else slice(0, 8)
            for y in range(8):
                sidebox[2 * which + s, y] = two(own[y][cols], own[y + 8][cols])
    pl.semaphore_wait(barrier, count)

    def request(n):
        return pltpu.make_async_remote_copy(
            src_ref=src_ref.at[other(n)], dst_ref=asked.at[me], send_sem=req_send.at[n], recv_sem=req_recv.at[n],
            device_id=(band, other(n)), device_id_type=MESH,
        )

    @pl.when(asks)
    def _():
        for n in range(1, PEERS + 1):
            request(n).start()
        asked[me] = src_ref[me]

    def halo(which, h):
        own = state_hbm if which == 0 else cot_hbm
        rows, sides, corners = ((frow, fside, fcorner), (crow, cside, ccorner))[which]
        src, dst = (
            (own.at[0:7], rows.at[1, 0:7]),
            (own.at[9:16], rows.at[0, 1:8]),
            (sidebox.at[2 * which + 1], sides.at[1]),
            (sidebox.at[2 * which], sides.at[0]),
            (cornerbox.at[2 * which + 1], corners.at[1]),
            (cornerbox.at[2 * which], corners.at[0]),
            (diagbox.at[2 * which + 1], corners.at[1, 0:4]),
            (diagbox.at[2 * which], corners.at[0, 0:4]),
        )[h]
        return pltpu.make_async_remote_copy(
            src_ref=src, dst_ref=dst, send_sem=halo_send.at[8 * which + h], recv_sem=halo_recv.at[8 * which + h],
            device_id=place(outward if h > 5 else HALO[h][0], HALO[h][1]), device_id_type=MESH,
        )

    def clean(x, ok):
        return jnp.where(ok, x.astype(F32), 0.0)

    def sends(h):
        return True if h < 4 else jnp.logical_not(edge) if h < 6 else beside

    def receives(h):
        return True if h < 4 else jnp.logical_not(edge) if h < 6 else edge

    def send_halo(which, hs):
        for h in hs:
            @pl.when(exists(*HALO[h]) & sends(h))
            def _(h=h):
                halo(which, h).start()

    def halo_arrived(which, hs):
        for h in hs:
            @pl.when(exists(-HALO[h][0], -HALO[h][1]) & receives(h))
            def _(h=h):
                halo(which, h).wait_recv()

    def halo_sent(which):
        for h in range(8):
            @pl.when(exists(*HALO[h]) & sends(h))
            def _(h=h):
                halo(which, h).wait_send()

    def send_corners(which):
        rows = frow if which == 0 else crow
        halo_arrived(which, (0, 1))
        for s in range(2):
            cols = slice(24, 32) if s == 0 else slice(0, 8)

            @pl.when(jnp.logical_not(edge))
            def _(s=s, cols=cols):
                for y in range(7):
                    cornerbox[2 * which + s, y] = two(rows[0, 1 + y][cols], rows[1, y][cols])

        send_halo(which, (4, 5))

    send_halo(0, (2, 3))
    send_halo(1, (2, 3))
    send_halo(0, (0, 1))
    send_halo(1, (0, 1))

    for here, top in ((band == 1, 0), (band == 6, 8)):
        @pl.when(here)
        def _(top=top):
            for which, own in ((0, state_ref), (1, cot_ref)):
                for s in range(2):
                    cols = slice(24, 32) if s == 0 else slice(0, 8)
                    for y in range(4):
                        diagbox[2 * which + s, y] = two(own[top + y][cols], own[top + y + 4][cols])

    send_halo(0, (6, 7))
    send_halo(1, (6, 7))

    loads[2].wait()
    loads[3].wait()
    for n in range(2):
        cols = slice(256 * n, 256 * n + 256)
        proj[:, cols] = dot(global_ref[...], cmap_ref[:, cols]).astype(BF)

    def send_row(n):
        return pltpu.make_async_remote_copy(
            src_ref=outbox.at[other(n)], dst_ref=fetched.at[me], send_sem=row_send.at[n], recv_sem=row_recv.at[n],
            device_id=(band, other(n)), device_id_type=MESH,
        )

    @pl.when(edge)
    def _():
        @pl.loop(0, 5)
        def _(t):
            group = [1 + 3 * t + u for u in range(3)]
            for n in group:
                request(n).wait_recv()
            hot = one_hot_rows(jnp.concatenate([asked[other(n)] for n in group], axis=1))
            rows = dot(hot, proj[...], ((0,), (0,))).astype(BF)
            for u, n in enumerate(group):
                outbox[other(n)] = rows[64 * u : 64 * u + 64]
                send_row(n).start()

    @pl.loop(1, PEERS + 1)
    def _(n):
        @pl.when(other_asks(n) & jnp.logical_not(edge))
        def _():
            request(n).wait_recv()
            hot = one_hot_rows(asked[other(n)])
            outbox[other(n)] = dot(hot, proj[...], ((0,), (0,))).astype(BF)
            send_row(n).start()

    @pl.when(asks)
    def _():
        fetched[me] = dot(one_hot_rows(asked[me]), proj[...], ((0,), (0,))).astype(BF)
        cell = lax.broadcasted_iota(jnp.int32, (512, 320), 0)
        hit = cell == bc_ref[...]
        relax = jnp.sum(w_ref[...], axis=0, keepdims=True)
        spread = jnp.sum(jnp.where(hit, relax, 0.0), axis=1, keepdims=True)
        keep_ref[...] = jnp.broadcast_to(1.0 - spread, (512, 128))
        hit = hit.astype(F32).astype(BF)

        def taps(m, carry):
            at = pl.ds(pl.multiple_of(m * 128, 128), 128)
            f = lax.broadcasted_iota(jnp.int32, (128, 320), 0) + m * 128
            total = jnp.zeros((128, 320), F32)
            for k in range(4):
                total = total + jnp.where(idx_ref[k : k + 1, :] == f, w_ref[k : k + 1, :], 0.0)
            bt[at, :] = total.astype(BF)
            return carry

        lax.fori_loop(0, 8, taps, 0)
        for m in range(2):
            at = slice(512 * m, 512 * m + 512)
            at_ref[at, :] = dot(bt[at, :], hit, ((1,), (1,))).astype(BF)
        for m in range(4):
            at = slice(256 * m, 256 * m + 256)
            amat[:, at] = dot(hit, bt[at, :], ((1,), (1,))).astype(BF)

    @pl.when(jnp.logical_not(asks))
    def _():
        keep_ref[...] = jnp.ones((512, 128), F32)

    loads[6].wait()
    for i in range(64):
        lined[:, i, :] = raw_ref[:, 64 * i : 64 * i + 64]
    for g in range(GROUPS):
        bias_ref[g] = lined[4 * g : 4 * g + 4].reshape(256, 64).T

    def spot(s):
        return slice(40, 48) if s == 0 else slice(32, 40)

    def build_own(ext, own):
        @pl.loop(0, 16, unroll=4)
        def _(y):
            ext[8 + y, 0:32] = own[y].astype(F32)

    def build_halo(ext, row, sides, corner):
        @pl.loop(0, 7)
        def _(y):
            ext[1 + y, 0:32] = clean(row[0, 1 + y], has[0])
            ext[24 + y, 0:32] = clean(row[1, y], has[1])

        @pl.when(jnp.logical_not(edge))
        def _():
            @pl.loop(0, 7)
            def _(y):
                for s in range(2):
                    both = clean(corner[s, y], has[2 + s])
                    ext[1 + y, spot(s)] = both[0:8]
                    ext[24 + y, spot(s)] = both[8:16]

        for here, v in ((band == 7, 0), (band == 0, 1)):
            @pl.when(here)
            def _(v=v):
                @pl.loop(0, 4)
                def _(y):
                    for s in range(2):
                        both = clean(corner[s, y], has[2 + s])
                        ext[24 * v + y, spot(s)] = both[0:8]
                        ext[24 * v + 4 + y, spot(s)] = both[8:16]
                        ext[24 * (1 - v) + y, spot(s)] = jnp.zeros((8, C), F32)
                        ext[24 * (1 - v) + 4 + y, spot(s)] = jnp.zeros((8, C), F32)

        @pl.loop(0, 8)
        def _(y):
            for s in range(2):
                both = clean(sides[s, y], has[2 + s])
                ext[8 + y, spot(s)] = both[0:8]
                ext[16 + y, spot(s)] = both[8:16]

    def to_windows(src, dst, wy, norm):
        for p in range(4):
            base = pl.multiple_of(wy * STRIP + p * 16, 16)
            r = oy + wy * 8 + p * 2
            rows = []
            for q in range(2):
                x = pltpu.roll(src[r + q], 8 - ox, 0)[0:40]
                if norm:
                    x = norm_rows(x)[0] * gain
                rows.append(x)
            for wx in range(WX):
                piece = jnp.concatenate([rows[0][8 * wx : 8 * wx + 8], rows[1][8 * wx : 8 * wx + 8]], axis=0)
                dst[pl.ds(pl.multiple_of(base + wx * 64, 16), 16), :] = piece.astype(BF)

    def project(first, windows):
        cells = pl.ds(pl.multiple_of(first * 64, 64), windows * 64)
        x = normed[cells, :]
        for n in range(6):
            cols = slice(256 * n, 256 * n + 256)
            qkv[cells, cols] = dot(x, wqkv_ref[:, cols]).astype(BF)

    def attend(pick, first, last):
        @pl.loop(first, last)
        def _(turn):
            items = []
            for u in range(UNROLL):
                wy, wx = pick(turn * UNROLL + u)
                cells = pl.ds(pl.multiple_of((wy * WX + wx) * 64, 64), 64)
                j = lax.broadcasted_iota(jnp.int32, (64, 1), 0)
                ry = band * 16 + oy - 8 + wy * 8 + j // 8
                rx = me * 32 + ox - 8 + wx * 8 + j % 8
                inside = (ry >= 0) & (ry < 128) & (rx >= 0) & (rx < 512)
                shut = jnp.where(inside, 0.0, -1e30)
                for g in range(GROUPS):
                    items.append((cells, shut, g, 128 * g))
            qs = [qkv[c, lo : lo + 128] for c, _, _, lo in items]
            ks = [qkv[c, 512 + lo : 512 + lo + 128] for c, _, _, lo in items]
            vs = [qkv[c, 1024 + lo : 1024 + lo + 128] for c, _, _, lo in items]
            qbs = [block_diagonal(q) for q in qs]
            gbs = [block_diagonal(gctx[c, lo : lo + 128]) for c, _, _, lo in items]
            ss = [dot(k, qb, ((1,), (1,))) for k, qb in zip(ks, qbs)]
            gps = [dot(v, gb, ((1,), (1,))) for v, gb in zip(vs, gbs)]
            pbs, gls = [], []
            for s, gp, (_, shut, g, _) in zip(ss, gps, items):
                s = s * SCALE + (bias_ref[g] + shut)
                e = jnp.exp(s - jnp.max(s, axis=0, keepdims=True))
                p = e * (1.0 / jnp.sum(e, axis=0, keepdims=True))
                gs = p * (gp - jnp.sum(p * gp, axis=0, keepdims=True))
                pbs.append(p.astype(BF))
                gls.append((gs * SCALE).astype(BF))
            a = [dot(pb, v, ((0,), (0,))) for pb, v in zip(pbs, vs)]
            b = [dot(gl, k, ((0,), (0,))) for gl, k in zip(gls, ks)]
            c = [dot(gl, qb) for gl, qb in zip(gls, qbs)]
            d = [dot(pb, gb) for pb, gb in zip(pbs, gbs)]
            for n, (cells, _, _, lo) in enumerate(items):
                ctx[cells, lo : lo + 128] = diagonal_blocks(a[n]).astype(BF)
                gqkv[cells, lo : lo + 128] = diagonal_blocks(b[n]).astype(BF)
                gqkv[cells, 512 + lo : 512 + lo + 128] = c[n].astype(BF)
                gqkv[cells, 1024 + lo : 1024 + lo + 128] = d[n].astype(BF)

    build_own(cext, cot_ref)
    send_corners(0)
    send_corners(1)

    @pl.when(asks)
    def _():
        @pl.loop(1, PEERS + 1)
        def _(n):
            send_row(n).wait_recv()

        for n in range(2):
            cols = slice(256 * n, 256 * n + 256)
            rows = jnp.concatenate([fetched[o, :, cols] for o in range(16)], axis=0)
            for y in range(4):
                at = slice(128 * y, 128 * y + 128)
                own = state_ref[4 * y : 4 * y + 4, :, cols].reshape(128, 256).astype(F32)
                x = own * keep_ref[at, 0:1] + dot(amat[at, :], rows)
                filled_ref[4 * y : 4 * y + 4, :, cols] = x.astype(BF).reshape(4, 32, 256)

    @pl.when(jnp.logical_not(asks))
    def _():
        filled_ref[...] = state_ref[...]

    def patch(n):
        s = n % 2
        if n < 2:
            dst, to = pside.at[s], place(0, 1 if s == 0 else -1)
        else:
            dst, to = prow.at[s], place(1 if s == 0 else -1, 0)
        return pltpu.make_async_remote_copy(
            src_ref=patchbox.at[n], dst_ref=dst, send_sem=patch_send.at[n], recv_sem=patch_recv.at[n],
            device_id=to, device_id_type=MESH,
        )

    PATCH = ((0, 1), (0, -1), (1, 0), (-1, 0))

    def patches(top, left, first):
        for s in range(2):
            if first == 0:
                y0, x0 = top, (24 if s == 0 else 0)
            else:
                y0, x0 = (8 if s == 0 else 0), left

            @pl.when(exists(*PATCH[first + s]))
            def _(n=first + s, y0=y0, x0=x0):
                for y in range(4):
                    patchbox[n, y] = two(filled_ref[y0 + y][x0 : x0 + 8], filled_ref[y0 + y + 4][x0 : x0 + 8])
                patch(n).start()

    for here, top in ((band == 0, 0), (band == 7, 8)):
        @pl.when(here)
        def _(top=top):
            patches(top, 0, 0)

    for here, left in ((me == 0, 0), (me == 15, 24)):
        @pl.when(here)
        def _(left=left):
            patches(0, left, 2)

    build_own(fext, filled_ref)
    loads[4].wait()
    loads[5].wait()
    halo_arrived(0, (2, 3, 4, 5, 6, 7))
    build_halo(fext, frow, fside, fcorner)
    halo_arrived(1, (2, 3, 4, 5, 6, 7))
    build_halo(cext, crow, cside, ccorner)

    @pl.loop(0, WY)
    def _(wy):
        to_windows(cext, cotw, wy, False)
        cells = pl.ds(pl.multiple_of(wy * STRIP, 64), STRIP)
        for n in range(2):
            cols = slice(256 * n, 256 * n + 256)
            gctx[cells, cols] = dot(cotw[cells, :], wout_ref[cols, :], ((1,), (1,))).astype(BF)

    for s in range(2):
        for here, top in ((band == 0, 0), (band == 7, 8)):
            @pl.when(here & has[2 + s])
            def _(s=s, top=top):
                patch(s).wait_recv()
                for y in range(4):
                    both = pside[s, y].astype(F32)
                    fext[8 + top + y, spot(s)] = both[0:8]
                    fext[12 + top + y, spot(s)] = both[8:16]
        for here, left in ((me == 0, 0), (me == 15, 24)):
            @pl.when(here & has[s])
            def _(s=s, left=left):
                patch(2 + s).wait_recv()
                for y in range(4):
                    both = prow[s, y].astype(F32)
                    fext[24 * s + y, left : left + 8] = both[0:8]
                    fext[24 * s + 4 + y, left : left + 8] = both[8:16]

    early = 2 * (1 - band // 4)
    start = 2 * (1 - me // 8)
    rest = 3 * (me // 8)
    first = 1 - early // 2

    @pl.loop(0, 2)
    def _(n):
        to_windows(fext, normed, first + n, True)
        project((first + n) * WX, WX)

    to_windows(fext, normed, early, True)
    project(early * WX + rest, 2)

    def late(n):
        last = n // 10
        wy = (1 - last) * (first + n // WX) + last * early
        wx = (1 - last) * lax.rem(n, WX) + last * (rest + n - 10)
        return wy, wx

    attend(late, 0, 4)

    def scatter(dst, wy, wx, windows, cols, x):
        for u in range(windows):
            for iy in range(8):
                at = 64 * u + 8 * iy
                dst[8 * wy + iy, pl.ds(pl.multiple_of(8 * (wx + u), 8), 8), cols] = x[at : at + 8]

    def input_gradient(wy, wx, windows):
        cells = pl.ds(pl.multiple_of((wy * WX + wx) * 64, 64), windows * 64)
        for n in range(2):
            cols = slice(256 * n, 256 * n + 256)
            scatter(gx, wy, wx, windows, cols, dot(gqkv[cells, :], wqkv_ref[cols, :], ((1,), (1,))))

    for iy in range(8):
        gx[8 * early + iy, pl.ds(pl.multiple_of(8 * start, 8), 24), :] = jnp.zeros((24, C), F32)

    @pl.loop(0, 2)
    def _(n):
        input_gradient(first + n, 0, WX)

    input_gradient(early, rest, 2)

    def norm_gradient(y):
        p = pltpu.roll(gx[y + 8 - oy], 32 + ox, 0)[0:32] * gain
        normal, inverse = norm_rows(filled_ref[y].astype(F32))
        g = inverse * (
            p - jnp.mean(p, axis=-1, keepdims=True) - normal * jnp.mean(p * normal, axis=-1, keepdims=True)
        )
        at = pl.ds(pl.multiple_of(y * 32, 32), 32)
        rgrad_ref[y] = (g * keep_ref[at, 0:1]).astype(BF)
        gfb[at, :] = g.astype(BF)

    pl.loop(0, 16, unroll=4)(norm_gradient)

    def send_back(n):
        return pltpu.make_async_remote_copy(
            src_ref=gfetch.at[other(n)], dst_ref=landed.at[me], send_sem=back_send.at[n], recv_sem=back_recv.at[n],
            device_id=(band, other(n)), device_id_type=MESH,
        )

    @pl.when(asks)
    def _():
        for k in (2, 1, 3, 0):
            plane = (me // 4) ^ k
            at = pl.ds(pl.multiple_of(256 * plane, 256), 256)
            for c in range(2):
                cols = slice(256 * c, 256 * c + 256)
                g = dot(at_ref[at, :], gfb[:, cols]).astype(BF)
                for o in range(4):
                    gfetch[4 * plane + o, :, cols] = g[64 * o : 64 * o + 64]
            for o in range(4):
                n = lax.rem((me ^ (4 * plane + o)) * 7, 16)

                @pl.when(n != 0)
                def _(n=n):
                    send_back(n).start()

    project(early * WX + start, 3)
    attend(lambda n: (early, start + n), 0, 1)
    input_gradient(early, start, 3)

    @pl.loop(0, 8, unroll=4)
    def _(y):
        norm_gradient(y + 4 * early)

    @pl.loop(0, WY)
    def _(wy):
        cells = pl.ds(pl.multiple_of(wy * STRIP, 64), STRIP)
        for n in range(2):
            cols = slice(256 * n, 256 * n + 256)
            scatter(upd, wy, 0, WX, cols, dot(ctx[cells, :], wout_ref[:, cols]))

    @pl.loop(0, 16, unroll=4)
    def _(y):
        update_ref[y] = pltpu.roll(upd[y + 8 - oy], 32 + ox, 0)[0:32].astype(BF)

    stores = [
        pltpu.make_async_copy(src, dst, store.at[n])
        for n, (src, dst) in enumerate(((update_ref, update_hbm), (rgrad_ref, rgrad_hbm), (ggrad_ref, ggrad_hbm)))
    ]
    stores[0].start()
    stores[1].start()
    summed[...] = jnp.zeros((256, C), F32)

    @pl.when(asks)
    def _():
        summed[...] = dot(one_hot_rows(asked[me]), gfetch[me])

    @pl.when(edge)
    def _():
        for t in range(3):
            group = [1 + 5 * t + u for u in range(5)]
            for n in group:
                send_back(n).wait_recv()
            hot = one_hot_rows(jnp.concatenate([asked[other(n)] for n in group], axis=1))
            for c in range(2):
                cols = slice(256 * c, 256 * c + 256)
                rows = jnp.concatenate([landed[other(n), :, cols] for n in group], axis=0)
                summed[:, cols] += dot(hot, rows)

    @pl.loop(1, PEERS + 1)
    def _(n):
        @pl.when(other_asks(n) & jnp.logical_not(edge))
        def _():
            send_back(n).wait_recv()
            summed[...] += dot(one_hot_rows(asked[other(n)]), landed[other(n)])

    total = summed[...]
    high = total.astype(BF)
    low = (total - high.astype(F32)).astype(BF)
    for n in range(4):
        at = slice(256 * n, 256 * n + 256)
        m = cmap_ref[at, :]
        ggrad_ref[:, at] = (dot(high, m, ((1,), (1,))) + dot(low, m, ((1,), (1,)))).astype(BF)

    stores[2].start()
    halo_sent(0)
    halo_sent(1)

    @pl.when(asks)
    def _():
        @pl.loop(1, PEERS + 1)
        def _(n):
            request(n).wait_send()
            send_back(n).wait_send()

    @pl.loop(1, PEERS + 1)
    def _(n):
        @pl.when(other_asks(n))
        def _():
            send_row(n).wait_send()

    for here, base in ((edge, 0), (side, 2)):
        for s in range(2):
            @pl.when(here & exists(*PATCH[base + s]))
            def _(n=base + s):
                patch(n).wait_send()

    for one in stores:
        one.wait()


def hand_over(*refs):
    sources, targets, held, (come, go) = refs[0:3], refs[3:6], refs[6:9], refs[9:11]
    moves = []
    for n in range(3):
        part = sources[n].shape[0] // 4
        for m in range(4):
            at = slice(m * part, m * part + part)
            moves.append((
                pltpu.make_async_copy(sources[n].at[at], held[n].at[at], come.at[4 * n + m]),
                pltpu.make_async_copy(held[n].at[at], targets[n].at[at], go.at[4 * n + m]),
            ))
    for one, _ in moves:
        one.start()
    for one, two_ in moves:
        one.wait()
        two_.start()
    for _, two_ in moves:
        two_.wait()


def shards(
    regional_state, global_state, boundary_cells, source_rows, interp_index, interp_weights, window_offsets,
    ln_gain, channel_map_weight, qkv_weight, out_weight, pos_bias, update_cot,
):
    idx = interp_index.reshape(320, 4).T
    w = interp_weights.reshape(320, 4).T
    vm = pl.BlockSpec(memory_space=pltpu.VMEM)
    hbm = pl.BlockSpec(memory_space=pl.ANY)
    smem = pl.BlockSpec(memory_space=pltpu.SMEM)
    v = pltpu.VMEM
    sems = pltpu.SemaphoreType.DMA
    update, rgrad, ggrad = pl.pallas_call(
        kernel,
        out_shape=(
            jax.ShapeDtypeStruct((16, 32, C), BF),
            jax.ShapeDtypeStruct((16, 32, C), BF),
            jax.ShapeDtypeStruct((256, 1024), BF),
        ),
        in_specs=[smem] + [vm] * 5 + [hbm] * 7,
        out_specs=(hbm, hbm, hbm),
        scratch_shapes=[
            v((16, 32, C), BF), v((16, 32, C), BF), v((256, 1024), BF),
            v((256, 1024), BF), v((1024, C), BF), v((16, 32, C), BF), v((16, 32, C), BF),
            v((C, 3 * C), BF), v((C, C), BF), v((HEADS, 4096), F32), v((HEADS, 64, 64), F32), v((4, 64, 256), F32),
            v((16, 1, 64), jnp.int32), v((16, 64, C), BF), v((16, 64, C), BF), v((256, C), BF),
            v((1024, 320), BF), v((512, 1024), BF), v((1024, 512), BF), v((512, 128), F32), v((16, 32, C), BF),
            v((4, 8, 16, C), BF), v((4, 7, 16, C), BF), v((4, 4, 16, C), BF), v((4, 4, 16, C), BF),
            v((2, 8, 32, C), BF), v((2, 8, 16, C), BF), v((2, 7, 16, C), BF),
            v((2, 8, 32, C), BF), v((2, 8, 16, C), BF), v((2, 7, 16, C), BF),
            v((2, 4, 16, C), BF), v((2, 4, 16, C), BF),
            v((32, 48, C), F32), v((32, 48, C), F32), v((960, C), BF), v((960, C), BF), v((960, 3 * C), BF),
            v((960, C), BF), v((960, C), BF), v((960, 3 * C), BF), v((24, 40, C), F32), v((24, 40, C), F32),
            v((512, C), BF), v((16, 64, C), BF), v((16, 64, C), BF), v((256, C), F32),
            sems((7,)), sems((3,)), sems((16,)), sems((16,)), sems((16,)), sems((16,)), sems((16,)), sems((16,)),
            sems((4,)), sems((4,)), sems((16,)), sems((16,)),
        ],
        compiler_params=pltpu.CompilerParams(
            collective_id=0, has_side_effects=True, vmem_limit_bytes=60 * 2**20
        ),
        cost_estimate=pl.CostEstimate(flops=8 * 10**9, bytes_accessed=8 * 10**6, transcendentals=10**6),
    )(
        window_offsets, source_rows.reshape(16, 1, 64), boundary_cells.reshape(1, 320), idx, w, ln_gain.reshape(1, C),
        global_state.reshape(256, 1024), channel_map_weight, regional_state, update_cot, qkv_weight, out_weight, pos_bias,
    )
    update, rgrad, ggrad = pl.pallas_call(
        hand_over,
        out_shape=(
            jax.ShapeDtypeStruct((16, 32, C), BF),
            jax.ShapeDtypeStruct((16, 32, C), BF),
            jax.ShapeDtypeStruct((256, 1024), BF),
        ),
        in_specs=[hbm] * 3,
        out_specs=(hbm,) * 3,
        scratch_shapes=[
            v((16, 32, C), BF), v((16, 32, C), BF), v((256, 1024), BF), sems((12,)), sems((12,)),
        ],
        compiler_params=pltpu.CompilerParams(vmem_limit_bytes=60 * 2**20),
    )(update, rgrad, ggrad)
    return update, rgrad, ggrad.reshape(16, 16, 1024)


def solution(mesh):
    tiled = P("band", "tile", None)
    deep = P("band", "tile", None, None)
    return jax.shard_map(
        shards,
        mesh=mesh,
        in_specs=(tiled, tiled, tiled, deep, deep, deep, P(), P(), P(), P(), P(), P(), tiled),
        out_specs=(tiled, tiled, tiled),
        check_vma=False,
    )
```

```python
import functools

import jax
import jax.numpy as jnp
from jax import lax
from jax.experimental import pallas as pl
from jax.experimental.pallas import tpu as pltpu
from jax.sharding import PartitionSpec as P

WS = 8
C = 512
HEADS = 16
GROUPS = 4
WY = 3
WX = 5
STRIP = WX * 64
EPS = 1e-05
BF = jnp.bfloat16
F32 = jnp.float32


def dot(a, b, dims=((1,), (0,))):
    return lax.dot_general(a, b, (dims, ((), ())), preferred_element_type=F32)


def norm_rows(x):
    centred = x - jnp.mean(x, axis=-1, keepdims=True)
    inverse = lax.rsqrt(jnp.mean(centred * centred, axis=-1, keepdims=True) + EPS)
    return centred * inverse, inverse


def block_diagonal(x):
    lane = lax.broadcasted_iota(jnp.int32, x.shape, 1) // 32
    return jnp.concatenate([jnp.where(lane == h, x, jnp.zeros_like(x)) for h in range(4)], axis=0)


def diagonal_blocks(x):
    lane = lax.broadcasted_iota(jnp.int32, (64, 128), 1) // 32
    out = x[192:256]
    for h in (2, 1, 0):
        out = jnp.where(lane == h, x[64 * h : 64 * h + 64], out)
    return out


MESH = pl.DeviceIdType.MESH
PEERS = 15
HALO = ((-1, 0), (1, 0), (0, -1), (0, 1), (0, -1), (0, 1), (0, -1), (0, 1))
UNROLL = 3
SCALE = 32 ** (-0.5)


def one_hot_rows(row):
    cell = lax.broadcasted_iota(jnp.int32, (256, row.shape[-1]), 0)
    return (cell == row).astype(F32).astype(BF)


def two(a, b):
    return jnp.concatenate([a.astype(F32), b.astype(F32)], axis=0).astype(BF)


def kernel(
    off_ref, src_ref, bc_ref, idx_ref, w_ref, gain_ref,
    global_hbm, cmap_hbm, state_hbm, cot_hbm, wqkv_hbm, wout_hbm, raw_hbm,
    update_hbm, rgrad_hbm, ggrad_hbm,
    update_ref, rgrad_ref, ggrad_ref,
    global_ref, cmap_ref, state_ref, cot_ref, wqkv_ref, wout_ref, raw_ref, lined, bias_ref,
    asked, fetched, outbox, proj, bt, amat, at_ref, keep_ref, filled_ref,
    sidebox, cornerbox, diagbox, patchbox, frow, fside, fcorner, crow, cside, ccorner, pside, prow,
    fext, cext, normed, cotw, qkv, gctx, ctx, gqkv, upd, gx, gfb, gfetch, landed, summed,
    load, store, req_send, req_recv, row_send, row_recv, halo_send, halo_recv, patch_send, patch_recv, back_send, back_recv,
):
    band, me = lax.axis_index("band"), lax.axis_index("tile")
    oy, ox = off_ref[0], off_ref[1]
    has = (band > 0, band < 7, me > 0, me < 15)
    edge = (band == 0) | (band == 7)
    side = (me == 0) | (me == 15)
    asks = edge | side
    beside = (band == 1) | (band == 6)
    outward = 2 * (band // 4) - 1
    gain = gain_ref[...]

    loads = [
        pltpu.make_async_copy(src, dst, load.at[n])
        for n, (src, dst) in enumerate((
            (state_hbm, state_ref), (cot_hbm, cot_ref), (global_hbm, global_ref), (cmap_hbm, cmap_ref),
            (wout_hbm, wout_ref), (wqkv_hbm, wqkv_ref), (raw_hbm, raw_ref),
        ))
    ]
    for one in loads:
        one.start()

    def place(dv, ds):
        return (lax.rem(band + 8 + dv, 8), lax.rem(me + 16 + ds, 16))

    def exists(dv, ds):
        ok = True
        if dv:
            ok = ok & (has[0] if dv < 0 else has[1])
        if ds:
            ok = ok & (has[2] if ds < 0 else has[3])
        return ok

    def other(n):
        return me ^ lax.rem(n * 7, 16)

    def other_asks(n):
        o = other(n)
        return edge | (o == 0) | (o == 15)

    barrier = pltpu.get_barrier_semaphore()
    for n in range(1, PEERS + 1):
        pl.semaphore_signal(barrier, inc=1, device_id=(band, other(n)), device_id_type=MESH)
    count = PEERS
    for dv, ds in HALO[0:2]:
        if dv:
            count = count + exists(dv, ds).astype(jnp.int32)

            @pl.when(exists(dv, ds))
            def _(dv=dv, ds=ds):
                pl.semaphore_signal(barrier, inc=1, device_id=place(dv, ds), device_id_type=MESH)
    for dv, here in ((1, (band == 0) | (band == 6)), (-1, (band == 1) | (band == 7))):
        for ds in (-1, 1):
            count = count + (here & exists(0, ds)).astype(jnp.int32)

            @pl.when(here & exists(0, ds))
            def _(dv=dv, ds=ds):
                pl.semaphore_signal(barrier, inc=1, device_id=place(dv, ds), device_id_type=MESH)
    for which, own in ((0, state_ref), (1, cot_ref)):
        loads[which].wait()
        for s in range(2):
            cols = slice(24, 32) if s == 0 else slice(0, 8)
            for y in range(8):
                sidebox[2 * which + s, y] = two(own[y][cols], own[y + 8][cols])
    pl.semaphore_wait(barrier, count)

    def request(n):
        return pltpu.make_async_remote_copy(
            src_ref=src_ref.at[other(n)], dst_ref=asked.at[me], send_sem=req_send.at[n], recv_sem=req_recv.at[n],
            device_id=(band, other(n)), device_id_type=MESH,
        )

    @pl.when(asks)
    def _():
        for n in range(1, PEERS + 1):
            request(n).start()
        asked[me] = src_ref[me]

    def halo(which, h):
        own = state_hbm if which == 0 else cot_hbm
        rows, sides, corners = ((frow, fside, fcorner), (crow, cside, ccorner))[which]
        src, dst = (
            (own.at[0:7], rows.at[1, 0:7]),
            (own.at[9:16], rows.at[0, 1:8]),
            (sidebox.at[2 * which + 1], sides.at[1]),
            (sidebox.at[2 * which], sides.at[0]),
            (cornerbox.at[2 * which + 1], corners.at[1]),
            (cornerbox.at[2 * which], corners.at[0]),
            (diagbox.at[2 * which + 1], corners.at[1, 0:4]),
            (diagbox.at[2 * which], corners.at[0, 0:4]),
        )[h]
        return pltpu.make_async_remote_copy(
            src_ref=src, dst_ref=dst, send_sem=halo_send.at[8 * which + h], recv_sem=halo_recv.at[8 * which + h],
            device_id=place(outward if h > 5 else HALO[h][0], HALO[h][1]), device_id_type=MESH,
        )

    def clean(x, ok):
        return jnp.where(ok, x.astype(F32), 0.0)

    def sends(h):
        return True if h < 4 else jnp.logical_not(edge) if h < 6 else beside

    def receives(h):
        return True if h < 4 else jnp.logical_not(edge) if h < 6 else edge

    def send_halo(which, hs):
        for h in hs:
            @pl.when(exists(*HALO[h]) & sends(h))
            def _(h=h):
                halo(which, h).start()

    def halo_arrived(which, hs):
        for h in hs:
            @pl.when(exists(-HALO[h][0], -HALO[h][1]) & receives(h))
            def _(h=h):
                halo(which, h).wait_recv()

    def halo_sent(which):
        for h in range(8):
            @pl.when(exists(*HALO[h]) & sends(h))
            def _(h=h):
                halo(which, h).wait_send()

    def send_corners(which):
        rows = frow if which == 0 else crow
        halo_arrived(which, (0, 1))
        for s in range(2):
            cols = slice(24, 32) if s == 0 else slice(0, 8)

            @pl.when(jnp.logical_not(edge))
            def _(s=s, cols=cols):
                for y in range(7):
                    cornerbox[2 * which + s, y] = two(rows[0, 1 + y][cols], rows[1, y][cols])

        send_halo(which, (4, 5))

    send_halo(0, (2, 3))
    send_halo(1, (2, 3))
    send_halo(0, (0, 1))
    send_halo(1, (0, 1))

    for here, top in ((band == 1, 0), (band == 6, 8)):
        @pl.when(here)
        def _(top=top):
            for which, own in ((0, state_ref), (1, cot_ref)):
                for s in range(2):
                    cols = slice(24, 32) if s == 0 else slice(0, 8)
                    for y in range(4):
                        diagbox[2 * which + s, y] = two(own[top + y][cols], own[top + y + 4][cols])

    send_halo(0, (6, 7))
    send_halo(1, (6, 7))

    loads[2].wait()
    loads[3].wait()
    for n in range(2):
        cols = slice(256 * n, 256 * n + 256)
        proj[:, cols] = dot(global_ref[...], cmap_ref[:, cols]).astype(BF)

    def send_row(n):
        return pltpu.make_async_remote_copy(
            src_ref=outbox.at[other(n)], dst_ref=fetched.at[me], send_sem=row_send.at[n], recv_sem=row_recv.at[n],
            device_id=(band, other(n)), device_id_type=MESH,
        )

    @pl.when(edge)
    def _():
        @pl.loop(0, 5)
        def _(t):
            group = [1 + 3 * t + u for u in range(3)]
            for n in group:
                request(n).wait_recv()
            hot = one_hot_rows(jnp.concatenate([asked[other(n)] for n in group], axis=1))
            rows = dot(hot, proj[...], ((0,), (0,))).astype(BF)
            for u, n in enumerate(group):
                outbox[other(n)] = rows[64 * u : 64 * u + 64]
                send_row(n).start()

    @pl.loop(1, PEERS + 1)
    def _(n):
        @pl.when(other_asks(n) & jnp.logical_not(edge))
        def _():
            request(n).wait_recv()
            hot = one_hot_rows(asked[other(n)])
            outbox[other(n)] = dot(hot, proj[...], ((0,), (0,))).astype(BF)
            send_row(n).start()

    @pl.when(asks)
    def _():
        fetched[me] = dot(one_hot_rows(asked[me]), proj[...], ((0,), (0,))).astype(BF)
        cell = lax.broadcasted_iota(jnp.int32, (512, 320), 0)
        hit = cell == bc_ref[...]
        relax = jnp.sum(w_ref[...], axis=0, keepdims=True)
        spread = jnp.sum(jnp.where(hit, relax, 0.0), axis=1, keepdims=True)
        keep_ref[...] = jnp.broadcast_to(1.0 - spread, (512, 128))
        hit = hit.astype(F32).astype(BF)

        def taps(m, carry):
            at = pl.ds(pl.multiple_of(m * 128, 128), 128)
            f = lax.broadcasted_iota(jnp.int32, (128, 320), 0) + m * 128
            total = jnp.zeros((128, 320), F32)
            for k in range(4):
                total = total + jnp.where(idx_ref[k : k + 1, :] == f, w_ref[k : k + 1, :], 0.0)
            bt[at, :] = total.astype(BF)
            return carry

        lax.fori_loop(0, 8, taps, 0)
        for m in range(2):
            at = slice(512 * m, 512 * m + 512)
            at_ref[at, :] = dot(bt[at, :], hit, ((1,), (1,))).astype(BF)
        for m in range(4):
            at = slice(256 * m, 256 * m + 256)
            amat[:, at] = dot(hit, bt[at, :], ((1,), (1,))).astype(BF)

    @pl.when(jnp.logical_not(asks))
    def _():
        keep_ref[...] = jnp.ones((512, 128), F32)

    loads[6].wait()
    for i in range(64):
        lined[:, i, :] = raw_ref[:, 64 * i : 64 * i + 64]
    for g in range(GROUPS):
        bias_ref[g] = lined[4 * g : 4 * g + 4].reshape(256, 64).T

    def spot(s):
        return slice(40, 48) if s == 0 else slice(32, 40)

    def build_own(ext, own):
        @pl.loop(0, 16, unroll=4)
        def _(y):
            ext[8 + y, 0:32] = own[y].astype(F32)

    def build_halo(ext, row, sides, corner):
        @pl.loop(0, 7)
        def _(y):
            ext[1 + y, 0:32] = clean(row[0, 1 + y], has[0])
            ext[24 + y, 0:32] = clean(row[1, y], has[1])

        @pl.when(jnp.logical_not(edge))
        def _():
            @pl.loop(0, 7)
            def _(y):
                for s in range(2):
                    both = clean(corner[s, y], has[2 + s])
                    ext[1 + y, spot(s)] = both[0:8]
                    ext[24 + y, spot(s)] = both[8:16]

        for here, v in ((band == 7, 0), (band == 0, 1)):
            @pl.when(here)
            def _(v=v):
                @pl.loop(0, 4)
                def _(y):
                    for s in range(2):
                        both = clean(corner[s, y], has[2 + s])
                        ext[24 * v + y, spot(s)] = both[0:8]
                        ext[24 * v + 4 + y, spot(s)] = both[8:16]
                        ext[24 * (1 - v) + y, spot(s)] = jnp.zeros((8, C), F32)
                        ext[24 * (1 - v) + 4 + y, spot(s)] = jnp.zeros((8, C), F32)

        @pl.loop(0, 8)
        def _(y):
            for s in range(2):
                both = clean(sides[s, y], has[2 + s])
                ext[8 + y, spot(s)] = both[0:8]
                ext[16 + y, spot(s)] = both[8:16]

    def to_windows(src, dst, wy, norm):
        for p in range(4):
            base = pl.multiple_of(wy * STRIP + p * 16, 16)
            r = oy + wy * 8 + p * 2
            rows = []
            for q in range(2):
                x = pltpu.roll(src[r + q], 8 - ox, 0)[0:40]
                if norm:
                    x = norm_rows(x)[0] * gain
                rows.append(x)
            for wx in range(WX):
                piece = jnp.concatenate([rows[0][8 * wx : 8 * wx + 8], rows[1][8 * wx : 8 * wx + 8]], axis=0)
                dst[pl.ds(pl.multiple_of(base + wx * 64, 16), 16), :] = piece.astype(BF)

    def project(first, windows):
        cells = pl.ds(pl.multiple_of(first * 64, 64), windows * 64)
        x = normed[cells, :]
        for n in range(6):
            cols = slice(256 * n, 256 * n + 256)
            qkv[cells, cols] = dot(x, wqkv_ref[:, cols]).astype(BF)

    def attend(pick, first, last):
        @pl.loop(first, last)
        def _(turn):
            items = []
            for u in range(UNROLL):
                wy, wx = pick(turn * UNROLL + u)
                cells = pl.ds(pl.multiple_of((wy * WX + wx) * 64, 64), 64)
                j = lax.broadcasted_iota(jnp.int32, (64, 1), 0)
                ry = band * 16 + oy - 8 + wy * 8 + j // 8
                rx = me * 32 + ox - 8 + wx * 8 + j % 8
                inside = (ry >= 0) & (ry < 128) & (rx >= 0) & (rx < 512)
                shut = jnp.where(inside, 0.0, -1e30)
                for g in range(GROUPS):
                    items.append((cells, shut, g, 128 * g))
            qs = [qkv[c, lo : lo + 128] for c, _, _, lo in items]
            ks = [qkv[c, 512 + lo : 512 + lo + 128] for c, _, _, lo in items]
            vs = [qkv[c, 1024 + lo : 1024 + lo + 128] for c, _, _, lo in items]
            qbs = [block_diagonal(q) for q in qs]
            gbs = [block_diagonal(gctx[c, lo : lo + 128]) for c, _, _, lo in items]
            ss = [dot(k, qb, ((1,), (1,))) for k, qb in zip(ks, qbs)]
            gps = [dot(v, gb, ((1,), (1,))) for v, gb in zip(vs, gbs)]
            pbs, gls = [], []
            for s, gp, (_, shut, g, _) in zip(ss, gps, items):
                s = s * SCALE + (bias_ref[g] + shut)
                e = jnp.exp(s - jnp.max(s, axis=0, keepdims=True))
                p = e * (1.0 / jnp.sum(e, axis=0, keepdims=True))
                gs = p * (gp - jnp.sum(p * gp, axis=0, keepdims=True))
                pbs.append(p.astype(BF))
                gls.append((gs * SCALE).astype(BF))
            a = [dot(pb, v, ((0,), (0,))) for pb, v in zip(pbs, vs)]
            b = [dot(gl, k, ((0,), (0,))) for gl, k in zip(gls, ks)]
            c = [dot(gl, qb) for gl, qb in zip(gls, qbs)]
            d = [dot(pb, gb) for pb, gb in zip(pbs, gbs)]
            for n, (cells, _, _, lo) in enumerate(items):
                ctx[cells, lo : lo + 128] = diagonal_blocks(a[n]).astype(BF)
                gqkv[cells, lo : lo + 128] = diagonal_blocks(b[n]).astype(BF)
                gqkv[cells, 512 + lo : 512 + lo + 128] = c[n].astype(BF)
                gqkv[cells, 1024 + lo : 1024 + lo + 128] = d[n].astype(BF)

    build_own(cext, cot_ref)
    send_corners(0)
    send_corners(1)

    @pl.when(asks)
    def _():
        @pl.loop(1, PEERS + 1)
        def _(n):
            send_row(n).wait_recv()

        for n in range(2):
            cols = slice(256 * n, 256 * n + 256)
            rows = jnp.concatenate([fetched[o, :, cols] for o in range(16)], axis=0)
            for y in range(4):
                at = slice(128 * y, 128 * y + 128)
                own = state_ref[4 * y : 4 * y + 4, :, cols].reshape(128, 256).astype(F32)
                x = own * keep_ref[at, 0:1] + dot(amat[at, :], rows)
                filled_ref[4 * y : 4 * y + 4, :, cols] = x.astype(BF).reshape(4, 32, 256)

    @pl.when(jnp.logical_not(asks))
    def _():
        filled_ref[...] = state_ref[...]

    def patch(n):
        s = n % 2
        if n < 2:
            dst, to = pside.at[s], place(0, 1 if s == 0 else -1)
        else:
            dst, to = prow.at[s], place(1 if s == 0 else -1, 0)
        return pltpu.make_async_remote_copy(
            src_ref=patchbox.at[n], dst_ref=dst, send_sem=patch_send.at[n], recv_sem=patch_recv.at[n],
            device_id=to, device_id_type=MESH,
        )

    PATCH = ((0, 1), (0, -1), (1, 0), (-1, 0))

    def patches(top, left, first):
        for s in range(2):
            if first == 0:
                y0, x0 = top, (24 if s == 0 else 0)
            else:
                y0, x0 = (8 if s == 0 else 0), left

            @pl.when(exists(*PATCH[first + s]))
            def _(n=first + s, y0=y0, x0=x0):
                for y in range(4):
                    patchbox[n, y] = two(filled_ref[y0 + y][x0 : x0 + 8], filled_ref[y0 + y + 4][x0 : x0 + 8])
                patch(n).start()

    for here, top in ((band == 0, 0), (band == 7, 8)):
        @pl.when(here)
        def _(top=top):
            patches(top, 0, 0)

    for here, left in ((me == 0, 0), (me == 15, 24)):
        @pl.when(here)
        def _(left=left):
            patches(0, left, 2)

    build_own(fext, filled_ref)
    loads[4].wait()
    loads[5].wait()
    halo_arrived(0, (2, 3, 4, 5, 6, 7))
    build_halo(fext, frow, fside, fcorner)
    halo_arrived(1, (2, 3, 4, 5, 6, 7))
    build_halo(cext, crow, cside, ccorner)

    @pl.loop(0, WY)
    def _(wy):
        to_windows(cext, cotw, wy, False)
        cells = pl.ds(pl.multiple_of(wy * STRIP, 64), STRIP)
        for n in range(2):
            cols = slice(256 * n, 256 * n + 256)
            gctx[cells, cols] = dot(cotw[cells, :], wout_ref[cols, :], ((1,), (1,))).astype(BF)

    for s in range(2):
        for here, top in ((band == 0, 0), (band == 7, 8)):
            @pl.when(here & has[2 + s])
            def _(s=s, top=top):
                patch(s).wait_recv()
                for y in range(4):
                    both = pside[s, y].astype(F32)
                    fext[8 + top + y, spot(s)] = both[0:8]
                    fext[12 + top + y, spot(s)] = both[8:16]
        for here, left in ((me == 0, 0), (me == 15, 24)):
            @pl.when(here & has[s])
            def _(s=s, left=left):
                patch(2 + s).wait_recv()
                for y in range(4):
                    both = prow[s, y].astype(F32)
                    fext[24 * s + y, left : left + 8] = both[0:8]
                    fext[24 * s + 4 + y, left : left + 8] = both[8:16]

    early = 2 * (1 - band // 4)
    start = 2 * (1 - me // 8)
    rest = 3 * (me // 8)
    first = 1 - early // 2

    @pl.loop(0, 2)
    def _(n):
        to_windows(fext, normed, first + n, True)
        project((first + n) * WX, WX)

    to_windows(fext, normed, early, True)
    project(early * WX + rest, 2)

    def late(n):
        last = n // 10
        wy = (1 - last) * (first + n // WX) + last * early
        wx = (1 - last) * lax.rem(n, WX) + last * (rest + n - 10)
        return wy, wx

    attend(late, 0, 4)

    def scatter(dst, wy, wx, windows, cols, x):
        for u in range(windows):
            for iy in range(8):
                at = 64 * u + 8 * iy
                dst[8 * wy + iy, pl.ds(pl.multiple_of(8 * (wx + u), 8), 8), cols] = x[at : at + 8]

    def input_gradient(wy, wx, windows):
        cells = pl.ds(pl.multiple_of((wy * WX + wx) * 64, 64), windows * 64)
        for n in range(2):
            cols = slice(256 * n, 256 * n + 256)
            scatter(gx, wy, wx, windows, cols, dot(gqkv[cells, :], wqkv_ref[cols, :], ((1,), (1,))))

    for iy in range(8):
        gx[8 * early + iy, pl.ds(pl.multiple_of(8 * start, 8), 24), :] = jnp.zeros((24, C), F32)

    @pl.loop(0, 2)
    def _(n):
        input_gradient(first + n, 0, WX)

    input_gradient(early, rest, 2)

    def norm_gradient(y):
        p = pltpu.roll(gx[y + 8 - oy], 32 + ox, 0)[0:32] * gain
        normal, inverse = norm_rows(filled_ref[y].astype(F32))
        g = inverse * (
            p - jnp.mean(p, axis=-1, keepdims=True) - normal * jnp.mean(p * normal, axis=-1, keepdims=True)
        )
        at = pl.ds(pl.multiple_of(y * 32, 32), 32)
        rgrad_ref[y] = (g * keep_ref[at, 0:1]).astype(BF)
        gfb[at, :] = g.astype(BF)

    pl.loop(0, 16, unroll=4)(norm_gradient)

    def send_back(n):
        return pltpu.make_async_remote_copy(
            src_ref=gfetch.at[other(n)], dst_ref=landed.at[me], send_sem=back_send.at[n], recv_sem=back_recv.at[n],
            device_id=(band, other(n)), device_id_type=MESH,
        )

    @pl.when(asks)
    def _():
        for pair in ((2, 1), (3, 0)):
            for k in pair:
                plane = (me // 4) ^ k
                at = pl.ds(pl.multiple_of(256 * plane, 256), 256)
                for c in range(2):
                    cols = slice(256 * c, 256 * c + 256)
                    g = dot(at_ref[at, :], gfb[:, cols]).astype(BF)
                    for o in range(4):
                        gfetch[4 * plane + o, :, cols] = g[64 * o : 64 * o + 64]
            for o in range(4):
                for k in pair:
                    d = 4 * k + (o ^ 2)
                    if d:
                        send_back(d * 7 % 16).start()

    project(early * WX + start, 3)
    attend(lambda n: (early, start + n), 0, 1)
    input_gradient(early, start, 3)

    @pl.loop(0, 8, unroll=4)
    def _(y):
        norm_gradient(y + 4 * early)

    @pl.loop(0, WY)
    def _(wy):
        cells = pl.ds(pl.multiple_of(wy * STRIP, 64), STRIP)
        for n in range(2):
            cols = slice(256 * n, 256 * n + 256)
            scatter(upd, wy, 0, WX, cols, dot(ctx[cells, :], wout_ref[:, cols]))

    @pl.loop(0, 16, unroll=4)
    def _(y):
        update_ref[y] = pltpu.roll(upd[y + 8 - oy], 32 + ox, 0)[0:32].astype(BF)

    stores = [
        pltpu.make_async_copy(src, dst, store.at[n])
        for n, (src, dst) in enumerate(((update_ref, update_hbm), (rgrad_ref, rgrad_hbm), (ggrad_ref, ggrad_hbm)))
    ]
    stores[0].start()
    stores[1].start()
    summed[...] = jnp.zeros((256, C), F32)

    @pl.when(asks)
    def _():
        summed[...] = dot(one_hot_rows(asked[me]), gfetch[me])

    @pl.when(edge)
    def _():
        for t in range(3):
            group = [1 + 5 * t + u for u in range(5)]
            for n in group:
                send_back(n).wait_recv()
            hot = one_hot_rows(jnp.concatenate([asked[other(n)] for n in group], axis=1))
            for c in range(2):
                cols = slice(256 * c, 256 * c + 256)
                rows = jnp.concatenate([landed[other(n), :, cols] for n in group], axis=0)
                summed[:, cols] += dot(hot, rows)

    @pl.loop(1, PEERS + 1)
    def _(n):
        @pl.when(other_asks(n) & jnp.logical_not(edge))
        def _():
            send_back(n).wait_recv()
            summed[...] += dot(one_hot_rows(asked[other(n)]), landed[other(n)])

    total = summed[...]
    high = total.astype(BF)
    low = (total - high.astype(F32)).astype(BF)
    for n in range(4):
        at = slice(256 * n, 256 * n + 256)
        m = cmap_ref[at, :]
        ggrad_ref[:, at] = (dot(high, m, ((1,), (1,))) + dot(low, m, ((1,), (1,)))).astype(BF)

    stores[2].start()
    halo_sent(0)
    halo_sent(1)

    @pl.when(asks)
    def _():
        @pl.loop(1, PEERS + 1)
        def _(n):
            request(n).wait_send()
            send_back(n).wait_send()

    @pl.loop(1, PEERS + 1)
    def _(n):
        @pl.when(other_asks(n))
        def _():
            send_row(n).wait_send()

    for here, base in ((edge, 0), (side, 2)):
        for s in range(2):
            @pl.when(here & exists(*PATCH[base + s]))
            def _(n=base + s):
                patch(n).wait_send()

    for one in stores:
        one.wait()


def hand_over(*refs):
    sources, targets, held, (come, go) = refs[0:3], refs[3:6], refs[6:9], refs[9:11]
    moves = []
    for n in range(3):
        part = sources[n].shape[0] // 4
        for m in range(4):
            at = slice(m * part, m * part + part)
            moves.append((
                pltpu.make_async_copy(sources[n].at[at], held[n].at[at], come.at[4 * n + m]),
                pltpu.make_async_copy(held[n].at[at], targets[n].at[at], go.at[4 * n + m]),
            ))
    for one, _ in moves:
        one.start()
    for one, two_ in moves:
        one.wait()
        two_.start()
    for _, two_ in moves:
        two_.wait()


def shards(
    regional_state, global_state, boundary_cells, source_rows, interp_index, interp_weights, window_offsets,
    ln_gain, channel_map_weight, qkv_weight, out_weight, pos_bias, update_cot,
):
    idx = interp_index.reshape(320, 4).T
    w = interp_weights.reshape(320, 4).T
    vm = pl.BlockSpec(memory_space=pltpu.VMEM)
    hbm = pl.BlockSpec(memory_space=pl.ANY)
    smem = pl.BlockSpec(memory_space=pltpu.SMEM)
    v = pltpu.VMEM
    sems = pltpu.SemaphoreType.DMA
    update, rgrad, ggrad = pl.pallas_call(
        kernel,
        out_shape=(
            jax.ShapeDtypeStruct((16, 32, C), BF),
            jax.ShapeDtypeStruct((16, 32, C), BF),
            jax.ShapeDtypeStruct((256, 1024), BF),
        ),
        in_specs=[smem] + [vm] * 5 + [hbm] * 7,
        out_specs=(hbm, hbm, hbm),
        scratch_shapes=[
            v((16, 32, C), BF), v((16, 32, C), BF), v((256, 1024), BF),
            v((256, 1024), BF), v((1024, C), BF), v((16, 32, C), BF), v((16, 32, C), BF),
            v((C, 3 * C), BF), v((C, C), BF), v((HEADS, 4096), F32), v((HEADS, 64, 64), F32), v((4, 64, 256), F32),
            v((16, 1, 64), jnp.int32), v((16, 64, C), BF), v((16, 64, C), BF), v((256, C), BF),
            v((1024, 320), BF), v((512, 1024), BF), v((1024, 512), BF), v((512, 128), F32), v((16, 32, C), BF),
            v((4, 8, 16, C), BF), v((4, 7, 16, C), BF), v((4, 4, 16, C), BF), v((4, 4, 16, C), BF),
            v((2, 8, 32, C), BF), v((2, 8, 16, C), BF), v((2, 7, 16, C), BF),
            v((2, 8, 32, C), BF), v((2, 8, 16, C), BF), v((2, 7, 16, C), BF),
            v((2, 4, 16, C), BF), v((2, 4, 16, C), BF),
            v((32, 48, C), F32), v((32, 48, C), F32), v((960, C), BF), v((960, C), BF), v((960, 3 * C), BF),
            v((960, C), BF), v((960, C), BF), v((960, 3 * C), BF), v((24, 40, C), F32), v((24, 40, C), F32),
            v((512, C), BF), v((16, 64, C), BF), v((16, 64, C), BF), v((256, C), F32),
            sems((7,)), sems((3,)), sems((16,)), sems((16,)), sems((16,)), sems((16,)), sems((16,)), sems((16,)),
            sems((4,)), sems((4,)), sems((16,)), sems((16,)),
        ],
        compiler_params=pltpu.CompilerParams(
            collective_id=0, has_side_effects=True, vmem_limit_bytes=60 * 2**20
        ),
        cost_estimate=pl.CostEstimate(flops=8 * 10**9, bytes_accessed=8 * 10**6, transcendentals=10**6),
    )(
        window_offsets, source_rows.reshape(16, 1, 64), boundary_cells.reshape(1, 320), idx, w, ln_gain.reshape(1, C),
        global_state.reshape(256, 1024), channel_map_weight, regional_state, update_cot, qkv_weight, out_weight, pos_bias,
    )
    update, rgrad, ggrad = pl.pallas_call(
        hand_over,
        out_shape=(
            jax.ShapeDtypeStruct((16, 32, C), BF),
            jax.ShapeDtypeStruct((16, 32, C), BF),
            jax.ShapeDtypeStruct((256, 1024), BF),
        ),
        in_specs=[hbm] * 3,
        out_specs=(hbm,) * 3,
        scratch_shapes=[
            v((16, 32, C), BF), v((16, 32, C), BF), v((256, 1024), BF), sems((12,)), sems((12,)),
        ],
        compiler_params=pltpu.CompilerParams(vmem_limit_bytes=60 * 2**20),
    )(update, rgrad, ggrad)
    return update, rgrad, ggrad.reshape(16, 16, 1024)


def solution(mesh):
    tiled = P("band", "tile", None)
    deep = P("band", "tile", None, None)
    return jax.shard_map(
        shards,
        mesh=mesh,
        in_specs=(tiled, tiled, tiled, deep, deep, deep, P(), P(), P(), P(), P(), P(), tiled),
        out_specs=(tiled, tiled, tiled),
        check_vma=False,
    )
```
